512 devices in a mesh: dp: 64 (over z_lo, x, y), fsdp: 8 (over z_hi, core).
Axes of the slice: x: 4, y: 4, z: 16 (z_hi: 4, z_lo: 4; z = z_hi * 4 + z_lo), core: 2. Of those that a mesh axis runs over, the one named last changes fastest.
Arguments:
- frames: bfloat16 [65536, 1536], P(('dp', 'fsdp')), may hold values from -6 to 6
- frame_mask: int32 [65536], P(('dp', 'fsdp')), may hold values 0 or 1
- block_dest: int32 [16384], P(('dp', 'fsdp')), may hold values from 0 to 63, as said below
- codes_first: int32 [1536, 24], P(None, 'fsdp'), may hold values from 0 to 255
- codes_second: int32 [1536, 24], P(None, 'fsdp'), may hold values from 0 to 255
- codebook_first: float32 [256, 128], replicated, may hold values from -0.15309311 to 0.15309311
- codebook_second: float32 [256, 128], replicated, may hold values from -0.07654656 to 0.07654656
- rotation: bfloat16 [1536, 1536], P('fsdp'), may hold values from -0.15625 to 0.15625
- gain: float32 [1536], replicated, may hold values from 0.25 to 1.75
- scale: float32 [3072], replicated, may hold values from 0.5 to 2
- cotangent: bfloat16 [65536, 3072], P(('dp', 'fsdp')), may hold values from -24 to 24
Outputs:
- activation: bfloat16 [65536, 3072], P(('dp', 'fsdp'))
- moved_frame_gradient: bfloat16 [65536, 1536], P(('dp', 'fsdp'))
- scale_grad: float32 [3072], P('fsdp')
- gain_grad: float32 [1536], replicated
The draws below stay inside these ranges and needn't reach their ends.
Inputs may be any that keep to these rules, and one draw needn't show every extreme that they name: `block_dest`: for every fsdp index and slot, the blocks of that slot on the 64 dp indices go to 64 different dp indices; the 32 blocks of one device go to different dp indices.
All inputs are finite; a program needn't handle non-finite values. No bound on the sum of `frame_mask` on one device may be relied on, other than what follows from the above.
Results may differ from the reference program's by a relative error of at most 0.0076.
Values may be sent and summed in bfloat16 or wider, within the bound.
A program may use at most 128 MiB of HBM per device.

```python
import math
import jax
import jax.numpy as jnp
from jax import lax

D = 1536
FF = 3072
CB = 256
QB = 128
BLK = 4
NB = 32
ROWS_DEV = 128
ROWS = 65536
N_DP = 64
N_FSDP = 8


def draw_block_dest(key, part):
    first, second = jax.random.split(key)
    order = jax.vmap(lambda k: jax.random.permutation(k, N_DP))(jax.random.split(first, N_FSDP)).astype(jnp.int32)
    shifts = jax.vmap(lambda k: jax.random.permutation(k, N_DP))(jax.random.split(second, N_FSDP)).astype(jnp.int32)[:, :NB]
    inverse = jnp.argsort(order, axis=1).astype(jnp.int32)
    target = (inverse[:, :, None] + shifts[:, None, :]) % N_DP
    picked = jnp.take_along_axis(order, target.reshape(N_FSDP, N_DP * NB), axis=1).reshape(N_FSDP, N_DP, NB)
    return jnp.transpose(picked, (1, 0, 2)).reshape(N_DP * N_FSDP * NB).astype(jnp.int32)


def set_ends(result, own_key, low, top_value):
    dims = result.shape
    place = [jax.random.randint(jax.random.fold_in(own_key, axis), (), 0, dims[axis]) for axis in range(len(dims))]
    result = result.at[tuple(place)].set(low)
    longest = dims.index(max(dims))
    place[longest] = (place[longest] + 1) % dims[longest]
    return result.at[tuple(place)].set(top_value)


def raised(result, own_key, source, target, parts, factor):
    def block_of(axis_at):
        return (jnp.arange(result.shape[axis_at]) // (result.shape[axis_at] // parts)).reshape((-1,) + (1,) * (result.ndim - 1 - axis_at))

    near = jax.random.permutation(own_key, parts)[block_of(target)]
    second = (block_of(target) + parts // 2) % parts
    return jnp.where((block_of(source) == near) | (block_of(source) == second), factor * result, result)


def block_scale(rng, dims, shards, smallest, largest):
    level = 1.0
    for position, blocks in shards:
        steps = jax.random.uniform(jax.random.fold_in(jax.random.fold_in(rng, 6), position), (blocks,), jnp.float32, smallest / len(shards), largest / len(shards))
        level = level * jnp.repeat(jnp.exp(steps), dims[position] // blocks).reshape((-1,) + (1,) * (len(dims) - 1 - position))
    return level


def centred(rng, shape, deviation, limit, shards=(), kind=jnp.bfloat16):
    entries = deviation * jax.random.normal(rng, shape, jnp.float32)
    if shards:
        entries = entries * block_scale(rng, shape, shards, -0.22, 0.18)
    return jnp.clip(entries, -limit, limit).astype(kind)


def noise_with(stream_key, shape, scale, reach, cuts, heavy, kind=jnp.bfloat16):
    drawn = scale * jax.random.normal(stream_key, shape, jnp.float32)
    if cuts:
        drawn = drawn * block_scale(stream_key, shape, cuts, -0.22, 0.18)
    return jnp.clip(raised(drawn, jax.random.fold_in(stream_key, 3), *heavy), -reach, reach).astype(kind)


def setup_inputs(seed: int = 0) -> dict:
    streams_of = jax.random.split(jax.random.key(seed), 12)
    return {
        "frames": centred(streams_of[0], (ROWS, D), 1.0, 6.0, ((0, 512),)),
        "frame_mask": set_ends((jax.random.randint(streams_of[1], (ROWS,), 0, 4) < 3).astype(jnp.int32), jax.random.fold_in(streams_of[1], 1), 0, 1),
        "block_dest": draw_block_dest(jax.random.fold_in(streams_of[11], 71), 0),
        "codes_first": set_ends(jax.random.randint(streams_of[3], (D, FF // QB), 0, CB), jax.random.fold_in(streams_of[3], 1), 0, CB - 1).astype(jnp.int32),
        "codes_second": set_ends(jax.random.randint(streams_of[4], (D, FF // QB), 0, CB), jax.random.fold_in(streams_of[4], 1), 0, CB - 1).astype(jnp.int32),
        "codebook_first": centred(streams_of[5], (CB, QB), (0.9 * D ** -0.5), 0.15309311, (), jnp.float32),
        "codebook_second": centred(streams_of[6], (CB, QB), (0.45 * D ** -0.5), 0.07654656, (), jnp.float32),
        "rotation": centred(streams_of[7], (D, D), D ** -0.5, 0.15625, ((0, 8),)),
        "gain": jnp.clip(1.0 + 0.15 * jax.random.normal(streams_of[8], (D,), jnp.float32), 0.25, 1.75),
        "scale": jnp.clip(jnp.exp(jax.random.uniform(streams_of[9], (FF,), jnp.float32, math.log(0.5), math.log(2.0))), 0.5, 2.0),
        "cotangent": noise_with(streams_of[10], (ROWS, FF), 1.0, 24.0, ((0, 512),), (0, 1, 512, 6.0)),
    }


def reference(frames, frame_mask, block_dest, codes_first, codes_second, codebook_first, codebook_second, rotation, gain, scale, cotangent):
    dest = block_dest.reshape(N_DP, N_FSDP, NB)
    fidx = jnp.arange(N_FSDP, dtype=jnp.int32)[None, :, None]
    sidx = jnp.arange(NB, dtype=jnp.int32)[None, None, :]
    kidx = jnp.broadcast_to(jnp.arange(N_DP, dtype=jnp.int32)[:, None, None], dest.shape)
    source = jnp.zeros(dest.shape, jnp.int32).at[dest, fidx, sidx].set(kidx)
    blocks = frames.reshape(N_DP, N_FSDP, NB, BLK, D)[source, fidx, sidx]
    masks = frame_mask.reshape(N_DP, N_FSDP, NB, BLK)[source, fidx, sidx]
    moved = blocks.reshape(N_DP * N_FSDP, ROWS_DEV, D)
    moved_mask = masks.reshape(N_DP * N_FSDP, ROWS_DEV)
    grads = cotangent.reshape(N_DP * N_FSDP, ROWS_DEV, FF)
    deq = jnp.take(codebook_first, codes_first, axis=0) + jnp.take(codebook_second, codes_second, axis=0)
    deq = deq.reshape(D, FF).astype(jnp.bfloat16)
    weight = jnp.dot(rotation, deq, preferred_element_type=jnp.float32).astype(jnp.bfloat16)

    def one_block(items):
        rows, mrow, grow = items
        xval = rows.astype(jnp.float32)
        centered_input = xval - lax.optimization_barrier(jnp.mean(xval, axis=1, keepdims=True))
        inverse_deviation = lax.rsqrt(lax.optimization_barrier(jnp.mean(centered_input * centered_input, axis=1, keepdims=True)) + 1e-06)
        standardized_input = centered_input * inverse_deviation
        normalized_output = (standardized_input * gain).astype(jnp.bfloat16)
        inner = jnp.dot(normalized_output, weight, preferred_element_type=jnp.float32)
        pre = inner * scale
        sig = jax.nn.sigmoid(pre)
        live = mrow.astype(jnp.float32)[:, None]
        activation = (pre * sig * live).astype(jnp.bfloat16)
        dpre = grow.astype(jnp.float32) * live * sig * (1.0 + pre * (1.0 - sig))
        scale_part = lax.optimization_barrier(jnp.sum(dpre * inner, axis=0))
        dinner = (dpre * scale).astype(jnp.bfloat16)
        normalized_gradient = jnp.dot(dinner, weight.T, preferred_element_type=jnp.float32)
        partial_gain_gradient = lax.optimization_barrier(jnp.sum(normalized_gradient * standardized_input, axis=0))
        standardized_gradient = normalized_gradient * gain
        moved_frame_gradient = inverse_deviation * (standardized_gradient - lax.optimization_barrier(jnp.mean(standardized_gradient, axis=1, keepdims=True)) - standardized_input * lax.optimization_barrier(jnp.mean(standardized_gradient * standardized_input, axis=1, keepdims=True)))
        return (activation, moved_frame_gradient.astype(jnp.bfloat16), scale_part, partial_gain_gradient)
    activation, moved_frame_gradient, scale_parts, gain_parts = lax.map(one_block, (moved, moved_mask, grads))
    return (activation.reshape(ROWS, FF), moved_frame_gradient.reshape(ROWS, D), lax.optimization_barrier(jnp.sum(scale_parts, axis=0)), lax.optimization_barrier(jnp.sum(gain_parts, axis=0)))
```

```python
import functools

import jax
import jax.numpy as jnp
from jax import lax
from jax.experimental import pallas as pl
from jax.experimental.pallas import tpu as pltpu
from jax.sharding import PartitionSpec as P

MESH = pl.DeviceIdType.MESH
F32 = jnp.float32
BF16 = jnp.bfloat16
NDP, NF = 64, 8
ROWS, D, FF = 128, 1536, 3072
SEG = 384
MSG = 16
PR, PC = 48, 384


def iota(shape, dim, dtype=jnp.int32):
    found = lax.broadcasted_iota(jnp.int32, shape, dim)
    return found if dtype == jnp.int32 else found.astype(dtype)


def kernel(
    frames, drow, mrow, cpk, cb1, cb2, rot, gain, scale, cot,
    act, mfg, red,
    outb, inb, wout, win, codes, turned, cbcat, rfull, deq, xhat, normed, ubuf, dinner, vbuf, dnorm,
    sbuf, gbuf, msg_a, got_a, msg_b, got_b, msg_c, got_c,
    s_frames, r_frames, s_meta, r_meta, s_own, s_code, r_code, s_codex, r_codex,
    s_r0, r_r0, s_r1, r_r1, s_r2, r_r2, s_rx, r_rx, s_red, r_red,
):
    dp = lax.axis_index("dp")
    fs = lax.axis_index("fsdp")
    zlo, xy = dp // 16, dp % 16
    xx, yy = xy // 4, xy % 4
    zhi, core = fs // 2, fs % 2
    other = zhi * 2 + 1 - core

    def to(src, dst, send, recv, d, f):
        return pltpu.make_async_remote_copy(
            src_ref=src, dst_ref=dst, send_sem=send, recv_sem=recv,
            device_id=(d, f), device_id_type=MESH,
        )

    def wait_for(ref, sem):
        pltpu.make_async_copy(ref, ref, sem).wait()

    barrier = pltpu.get_barrier_semaphore()

    def hello_dp(j, _):
        pl.semaphore_signal(barrier, inc=1, device_id=((dp + j) % NDP, fs), device_id_type=MESH)
        return 0

    def hello_fs(j, _):
        pl.semaphore_signal(barrier, inc=1, device_id=(dp, (fs + j) % NF), device_id_type=MESH)
        return 0

    lax.fori_loop(1, NDP, hello_dp, 0)
    lax.fori_loop(1, NF, hello_fs, 0)

    lane = iota((1, ROWS), 1)
    dest = drow[...]
    key = jnp.concatenate([dest * MSG + s * 4 + lane % 4 for s in range(4)], axis=1)
    wide = jnp.concatenate([frames[:, s * SEG : (s + 1) * SEG] for s in range(4)], axis=0)

    def fill(k, _):
        row = iota((256, 4 * ROWS), 0) + k * 256
        pick = jnp.where(row == key, 1.0, 0.0).astype(BF16)
        outb[pl.ds(pl.multiple_of(k * 256, 256), 256), :] = jnp.dot(
            pick, wide, preferred_element_type=F32
        ).astype(BF16)
        return 0

    lax.fori_loop(0, 4, fill, 0)
    wout[...] = jnp.where(iota((NDP, 1, ROWS), 0) == dest[None], 1.0 + mrow[...][None], 0.0)

    for k, book in enumerate((cb1, cb2)):
        value = book[...]
        high = value.astype(BF16)
        cbcat[k * 256 : (k + 1) * 256, 0:128] = high
        cbcat[k * 256 : (k + 1) * 256, 128:256] = (value - high.astype(F32)).astype(BF16)
    codes[fs] = cpk[...]
    rfull[pl.ds(pl.multiple_of(fs * 192, 192), 192), :] = rot[...]
    win[dp] = wout[dp]

    pl.semaphore_wait(barrier, NDP - 1 + NF - 1)

    def rows_of(f):
        return pl.ds(pl.multiple_of(f * 192, 192), 192)

    def piece(f, i, j):
        return rfull.at[
            pl.ds(pl.multiple_of(f * 192 + i * PR, 16), PR), pl.ds(pl.multiple_of(j * PC, 128), PC)
        ]

    def away(k):
        return ((zhi + k) % 4) * 2 + core

    def back(k):
        return ((zhi + 4 - k) % 4) * 2 + core

    for k in (1, 2, 3):
        to(cpk, codes.at[fs], s_code.at[k - 1], r_code.at[k - 1], dp, away(k)).start()
    to(cpk, codes.at[fs], s_codex.at[0], r_codex.at[0], dp, other).start()
    for k in (1, 2, 3):
        to(piece(fs, xx, yy), piece(fs, xx, yy), s_r0.at[k - 1], r_r0.at[k - 1], dp, away(k)).start()
    to(rfull.at[rows_of(fs), :], rfull.at[rows_of(fs), :], s_rx.at[0], r_rx.at[0], dp, other).start()

    def block(c):
        return pl.ds(pl.multiple_of(c * MSG, MSG), MSG)

    def send_block(j, _):
        peer = (dp + j) % NDP
        to(wout.at[peer], win.at[dp], s_meta, r_meta, peer, fs).start()
        to(outb.at[block(peer), :], inb.at[block(dp), :], s_frames, r_frames, peer, fs).start()
        return 0

    lax.fori_loop(1, NDP, send_block, 0)
    own = pltpu.make_async_copy(outb.at[block(dp), :], inb.at[block(dp), :], s_own)
    own.start()

    def look_up(f):
        part = jnp.concatenate([codes[f].astype(F32), jnp.zeros((32, 128), F32)], axis=0)
        turned[...] = part.T
        entry = iota((128, 256), 1, F32)

        def step(t, _):
            table = turned[...]
            hot = jnp.concatenate(
                [
                    jnp.concatenate(
                        [
                            jnp.where(table[:, h * 8 + b * 3 + q : h * 8 + b * 3 + q + 1] == entry, 1.0, 0.0).astype(BF16)
                            for b in range(2)
                        ],
                        axis=1,
                    )
                    for h in range(2)
                    for q in range(3)
                ],
                axis=0,
            )
            found = jnp.dot(hot, cbcat[...], preferred_element_type=F32)
            found = (found[:, :128] + found[:, 128:]).astype(BF16)
            for h in range(2):
                for q in range(3):
                    deq[
                        pl.ds(pl.multiple_of(t * 256 + h * 128, 128), 128),
                        pl.ds(pl.multiple_of(f * 384 + q * 128, 128), 128),
                    ] = found[(h * 3 + q) * 128 : (h * 3 + q + 1) * 128, :]
            turned[...] = pltpu.roll(table, 112, 1)
            return 0

        lax.fori_loop(0, 6, step, 0)

    look_up(fs)

    for k in (1, 2, 3):
        wait_for(codes.at[back(k)], r_code.at[k - 1])
        to(codes.at[back(k)], codes.at[back(k)], s_codex.at[k], r_codex.at[k], dp, other).start()
    for k in (1, 2, 3):
        wait_for(piece(back(k), xx, yy), r_r0.at[k - 1])
        for d in (1, 2, 3):
            nx = (xx + d * (1 - core)) % 4
            ny = (yy + d * core) % 4
            to(piece(back(k), xx, yy), piece(back(k), xx, yy), s_r1, r_r1.at[k - 1], zlo * 16 + nx * 4 + ny, fs).start()

    wait_for(codes.at[other], r_codex.at[0])
    look_up(other)
    look_up(back(1))

    for k in (1, 2, 3):
        wait_for(rfull.at[0:144, 0:PC], r_r1.at[k - 1])

        def spread(n, _):
            d, m = n // 4 + 1, n % 4
            nx = (xx + d * core) % 4
            ny = (yy + d * (1 - core)) % 4
            px = m * (1 - core) + xx * core
            py = yy * (1 - core) + m * core
            to(piece(back(k), px, py), piece(back(k), px, py), s_r2, r_r2.at[k - 1], zlo * 16 + nx * 4 + ny, fs).start()
            return 0

        lax.fori_loop(0, 12, spread, 0)

    look_up(back(2))
    look_up(back(3))
    for k in (1, 2, 3):
        wait_for(codes.at[back(k)], r_codex.at[k])

    def other_of(f):
        return f + 1 - 2 * core

    look_up(other_of(back(1)))

    for k in (1, 2, 3):
        wait_for(rfull.at[0:576, 0:PC], r_r2.at[k - 1])
        to(rfull.at[rows_of(back(k)), :], rfull.at[rows_of(back(k)), :], s_rx.at[k], r_rx.at[k], dp, other).start()

    look_up(other_of(back(2)))
    look_up(other_of(back(3)))

    wait_for(win.at[0 : NDP - 1], r_meta)
    wait_for(inb.at[0 : (NDP - 1) * MSG, :], r_frames)
    own.wait()
    meta = win[...]
    mask_row = jnp.sum(meta, axis=0) - 1.0
    src_row = jnp.sum(jnp.where(meta > 0.5, iota((NDP, 1, ROWS), 0, F32), 0.0), axis=0)
    eye = iota((ROWS, ROWS), 0) == iota((ROWS, ROWS), 1)
    live = jnp.sum(jnp.where(eye, mask_row, 0.0), axis=1, keepdims=True)
    src = jnp.sum(jnp.where(eye, src_row, 0.0), axis=1, keepdims=True)
    first = src * float(MSG) + (iota((ROWS, 1), 0) % 4).astype(F32)
    for s in range(4):
        put = jnp.where(iota((ROWS, NDP * MSG), 1, F32) == first + 4.0 * s, 1.0, 0.0).astype(BF16)
        xhat[:, s * SEG : (s + 1) * SEG] = jnp.dot(put, inb[...], preferred_element_type=F32)
    xval = xhat[...]
    centered = xval - jnp.sum(xval, axis=1, keepdims=True) * (1.0 / D)
    inv = lax.rsqrt(jnp.sum(centered * centered, axis=1, keepdims=True) * (1.0 / D) + 1e-06)
    standard = centered * inv
    xhat[...] = standard
    normed[...] = (standard * gain[...]).astype(BF16)

    for k in range(4):
        wait_for(rfull.at[rows_of(other_of(back(k))), :], r_rx.at[k])

    def forward_u(n, _):
        cols = pl.ds(pl.multiple_of(n * 512, 512), 512)
        ubuf[:, cols] = jnp.dot(normed[...], rfull[:, cols], preferred_element_type=F32).astype(BF16)
        return 0

    lax.fori_loop(0, 3, forward_u, 0)

    sbuf[...] = jnp.zeros_like(sbuf)
    gbuf[...] = jnp.zeros_like(gbuf)

    def forward(n, _):
        cols = pl.ds(pl.multiple_of(n * 768, 768), 768)
        inner = jnp.dot(ubuf[...], deq[:, cols], preferred_element_type=F32)
        sc = scale[:, cols]
        pre = inner * sc
        sig = 1.0 / (1.0 + jnp.exp(-pre))
        act[:, cols] = (pre * sig * live).astype(BF16)
        dpre = cot[:, cols].astype(F32) * live * sig * (1.0 + pre * (1.0 - sig))
        part = jnp.sum(dpre * inner, axis=0, keepdims=True)
        for h in range(2):
            for r in range(3):
                at = h * 384 + r * 128
                sbuf[n * 2 + h, r : r + 1, :] = part[:, at : at + 128]
        dinner[:, cols] = (dpre * sc).astype(BF16)
        return 0

    lax.fori_loop(0, 4, forward, 0)

    nt = (((1,), (1,)), ((), ()))

    def backward_v(n, _):
        rows = pl.ds(pl.multiple_of(n * 256, 256), 256)
        vbuf[:, rows] = lax.dot_general(dinner[...], deq[rows, :], nt, preferred_element_type=F32).astype(BF16)
        return 0

    lax.fori_loop(0, 6, backward_v, 0)

    def backward_n(n, _):
        rows = pl.ds(pl.multiple_of(n * 512, 512), 512)
        dnorm[:, rows] = lax.dot_general(vbuf[...], rfull[rows, :], nt, preferred_element_type=F32)
        return 0

    lax.fori_loop(0, 3, backward_n, 0)

    dn = dnorm[...]
    xh = xhat[...]
    gpart = jnp.sum(dn * xh, axis=0, keepdims=True)
    for r in range(12):
        gbuf[3 + r : 4 + r, :] = gpart[:, r * 128 : (r + 1) * 128]
    msg_a[...] = sbuf[...] + gbuf[...][None]
    got_a[fs] = msg_a[fs]

    def red_a(j, _):
        pf = (fs + j) % NF
        to(msg_a.at[pf], got_a.at[fs], s_red.at[0], r_red.at[0], dp, pf).start()
        return 0

    lax.fori_loop(1, NF, red_a, 0)

    dx = dn * gain[...]
    m1 = jnp.sum(dx, axis=1, keepdims=True) * (1.0 / D)
    m2 = jnp.sum(dx * xh, axis=1, keepdims=True) * (1.0 / D)
    mfg[...] = (inv * (dx - m1 - xh * m2)).astype(BF16)

    wait_for(got_a.at[0 : NF - 1], r_red.at[0])
    total = jnp.sum(got_a[...], axis=0)
    msg_b[...] = total
    got_b[xy] = total

    def red_b(j, _):
        to(msg_b, got_b.at[xy], s_red.at[1], r_red.at[1], zlo * 16 + (xy + j) % 16, fs).start()
        return 0

    lax.fori_loop(1, 16, red_b, 0)
    wait_for(got_b.at[0:15], r_red.at[1])
    total = jnp.sum(got_b[...], axis=0)
    msg_c[...] = total
    got_c[zlo] = total
    for j in (1, 2, 3):
        to(msg_c, got_c.at[zlo], s_red.at[2], r_red.at[2], ((zlo + j) % 4) * 16 + xy, fs).start()
    wait_for(got_c.at[0:3], r_red.at[2])
    red[...] = jnp.sum(got_c[...], axis=0)

    wait_for(outb.at[0 : (NDP - 1) * MSG, :], s_frames)
    wait_for(wout.at[0 : NDP - 1], s_meta)
    for k in range(3):
        wait_for(cpk, s_code.at[k])
        wait_for(piece(fs, xx, yy), s_r0.at[k])
    for k in range(4):
        wait_for(cpk, s_codex.at[k])
        wait_for(rfull.at[0:192, :], s_rx.at[k])
    wait_for(rfull.at[0:432, 0:PC], s_r1)
    wait_for(rfull.at[0:432, :], s_r2)
    wait_for(got_a.at[0 : NF - 1], s_red.at[0])
    wait_for(got_b.at[0:15], s_red.at[1])
    wait_for(got_c.at[0:3], s_red.at[2])


def body(
    frames, frame_mask, block_dest, codes_first, codes_second, codebook_first, codebook_second,
    rotation, gain, scale, cotangent,
):
    drow = jnp.repeat(block_dest, 4)[None, :]
    mrow = frame_mask.astype(F32)[None, :]
    both = jnp.concatenate([codes_first.T, codes_second.T, jnp.zeros((2, D), jnp.int32)], axis=0)
    cpk = both.astype(BF16).reshape(8, 12, 128).transpose(1, 0, 2).reshape(96, 128)
    dma = pltpu.SemaphoreType.DMA
    vm = pltpu.VMEM
    act, mfg, red = pl.pallas_call(
        kernel,
        out_shape=(
            jax.ShapeDtypeStruct((ROWS, FF), BF16),
            jax.ShapeDtypeStruct((ROWS, D), BF16),
            jax.ShapeDtypeStruct((16, 128), F32),
        ),
        in_specs=[pl.BlockSpec(memory_space=pltpu.VMEM)] * 10,
        out_specs=(pl.BlockSpec(memory_space=pltpu.VMEM),) * 3,
        scratch_shapes=[
            vm((NDP * MSG, SEG), BF16), vm((NDP * MSG, SEG), BF16),
            vm((NDP, 1, ROWS), F32), vm((NDP, 1, ROWS), F32),
            vm((NF, 96, 128), BF16), vm((128, 128), F32), vm((512, 256), BF16),
            vm((D, D), BF16), vm((D, FF), BF16),
            vm((ROWS, D), F32), vm((ROWS, D), BF16), vm((ROWS, D), BF16),
            vm((ROWS, FF), BF16), vm((ROWS, D), BF16), vm((ROWS, D), F32),
            vm((NF, 16, 128), F32), vm((16, 128), F32),
            vm((NF, 16, 128), F32), vm((NF, 16, 128), F32),
            vm((16, 128), F32), vm((16, 16, 128), F32),
            vm((16, 128), F32), vm((4, 16, 128), F32),
            dma, dma, dma, dma, dma,
            dma((3,)), dma((3,)), dma((4,)), dma((4,)),
            dma((3,)), dma((3,)), dma, dma((3,)), dma, dma((3,)), dma((4,)), dma((4,)),
            dma((3,)), dma((3,)),
        ],
        compiler_params=pltpu.CompilerParams(
            collective_id=0, has_side_effects=True, vmem_limit_bytes=52 * 1024 * 1024
        ),
        cost_estimate=pl.CostEstimate(flops=14_000_000_000, bytes_accessed=8_000_000, transcendentals=400_000),
    )(
        frames, drow, mrow, cpk, codebook_first, codebook_second, rotation,
        gain[None, :], scale[None, :], cotangent,
    )
    return act, mfg, red[0:3].reshape(384), red[3:15].reshape(D)


def solution(mesh):
    rows = P(("dp", "fsdp"), None)
    flat = P(("dp", "fsdp"))
    placed = (
        rows, flat, flat, P(None, "fsdp"), P(None, "fsdp"), P(), P(), P("fsdp", None), P(), P(), rows,
    )
    return jax.shard_map(
        body,
        mesh=mesh,
        in_specs=placed,
        out_specs=(rows, rows, P("fsdp"), P()),
        check_vma=False,
    )
```

```python
import jax
import jax.numpy as jnp
from jax import lax
from jax.experimental import pallas as pl
from jax.experimental.pallas import tpu as pltpu
from jax.sharding import PartitionSpec as P

MESH = pl.DeviceIdType.MESH
F32 = jnp.float32
BF16 = jnp.bfloat16
NDP, NF = 64, 8
ROWS, D, FF = 128, 1536, 3072
SEG = 384
MSG = 16
PR, PC = 48, 384
HALF = D // 2
WIDE = 768


def iota(shape, dim, dtype=jnp.int32):
    found = lax.broadcasted_iota(jnp.int32, shape, dim)
    return found if dtype == jnp.int32 else found.astype(dtype)


def kernel(
    frames_h, mask_h, dest_h, c1_h, c2_h, cb1_h, cb2_h, rot_h, gain_h, scale_h, cot_h,
    act_h, mfg_h, sred, gred,
    frames, mask, destv, c1, c2, cb1, cb2, gain, scale, cot, act, mfg,
    outb, inb, wout, win, codef, codes, cbcat, rfull, deq, xhat, normed, ubuf, vacc, vbuf, dnorm,
    sbuf, sgot, smsg_b, sgot_b, smsg_c, sgot_c, ghalf, ggot, gmsg_z, ggot_z, gmsg_x, ggot_x, gfin,
    s_in, s_out, s_frames, r_frames, s_meta, r_meta, s_own, s_c0, r_c0, s_c1, r_c1,
    s_r0, r_r0, s_r1, r_r1, s_r2, r_r2, s_rx, r_rx, s_dx, r_dx, s_red, r_red,
):
    dp = lax.axis_index("dp")
    fs = lax.axis_index("fsdp")
    zlo, xy = dp // 16, dp % 16
    xx, yy = xy // 4, xy % 4
    zhi, core = fs // 2, fs % 2
    zz = zhi * 4 + zlo
    other = zhi * 2 + 1 - core

    def to(src, dst, send, recv, d, f):
        return pltpu.make_async_remote_copy(
            src_ref=src, dst_ref=dst, send_sem=send, recv_sem=recv,
            device_id=(d, f), device_id_type=MESH,
        )

    def wait_for(ref, sem):
        pltpu.make_async_copy(ref, ref, sem).wait()

    def rows_of(f):
        return pl.ds(pl.multiple_of(f * 192, 192), 192)

    def cols_of(f):
        return pl.ds(pl.multiple_of(f * SEG, SEG), SEG)

    pairs = (
        (dest_h, destv), (mask_h, mask), (frames_h, frames), (c1_h, c1), (c2_h, c2), (cb1_h, cb1), (cb2_h, cb2),
        (gain_h, gain), (scale_h, scale), (cot_h, cot), (rot_h, rfull.at[rows_of(fs), :]),
    )
    loads = [pltpu.make_async_copy(a, b, s_in.at[n]) for n, (a, b) in enumerate(pairs)]
    for load in loads:
        load.start()

    barrier = pltpu.get_barrier_semaphore()

    def greet(d, f):
        pl.semaphore_signal(barrier, inc=1, device_id=(d, f), device_id_type=MESH)

    def hello_dp(j, _):
        greet((dp + j) % NDP, fs)
        return 0

    def hello_fs(j, _):
        greet(dp, (fs + j) % NF)
        return 0

    def hello_z(j, _):
        greet(((zlo + 1 + j % 3) % 4) * 16 + xy, ((zhi + 1 + j // 3) % 4) * 2 + core)
        return 0

    lax.fori_loop(1, NF, hello_fs, 0)
    lax.fori_loop(1, NDP, hello_dp, 0)
    lax.fori_loop(0, 9, hello_z, 0)

    codef[...] = jnp.zeros_like(codef)
    loads[3].wait()
    loads[4].wait()
    for t in range(12):
        codef[t * 8 : t * 8 + 3, :] = c1[:, t * 128 : (t + 1) * 128].astype(F32)
        codef[t * 8 + 3 : t * 8 + 6, :] = c2[:, t * 128 : (t + 1) * 128].astype(F32)
    codes[fs] = codef[...].astype(BF16)

    loads[0].wait()
    loads[1].wait()
    spread4 = jnp.where(iota((32, ROWS), 1) // 4 == iota((32, ROWS), 0), 1.0, 0.0).astype(BF16)
    dest8 = jnp.broadcast_to(destv[...].reshape(1, 32).astype(F32), (8, 32)).astype(BF16)
    dest = jnp.dot(dest8, spread4, preferred_element_type=F32)[0:1, :].astype(jnp.int32)
    mask_in = mask[...].reshape(1, ROWS).astype(F32)
    lane = iota((1, ROWS), 1)
    key = jnp.concatenate([dest * MSG + s * 4 + lane % 4 for s in range(4)], axis=1)
    wout[...] = jnp.where(iota((NDP, 1, ROWS), 0) == dest[None], 1.0 + mask_in[None], 0.0)
    win[dp] = wout[dp]
    loads[2].wait()
    wide = jnp.concatenate([frames[:, s * SEG : (s + 1) * SEG] for s in range(4)], axis=0)

    def fill(k, _):
        row = iota((256, 4 * ROWS), 0) + k * 256
        pick = jnp.where(row == key, 1.0, 0.0).astype(BF16)
        outb[pl.ds(pl.multiple_of(k * 256, 256), 256), :] = jnp.dot(
            pick, wide, preferred_element_type=F32
        ).astype(BF16)
        return 0

    lax.fori_loop(0, 4, fill, 0)

    pl.semaphore_wait(barrier, NDP - 1 + NF - 1 + 9)

    def piece(f, i, j):
        return rfull.at[
            pl.ds(pl.multiple_of(f * 192 + i * PR, 16), PR), pl.ds(pl.multiple_of(j * PC, 128), PC)
        ]

    def own_piece(i, j):
        return rot_h.at[pl.ds(pl.multiple_of(i * PR, 16), PR), pl.ds(pl.multiple_of(j * PC, 128), PC)]

    def code_piece(f, i):
        return codes.at[f, pl.ds(pl.multiple_of(i * 32, 32), 32), :]

    def away(k):
        return ((zhi + k) % 4) * 2 + core

    def back(k):
        return ((zhi + 4 - k) % 4) * 2 + core

    def other_of(f):
        return f + 1 - 2 * core

    for k in (1, 2, 3):
        to(code_piece(fs, xx), code_piece(fs, xx), s_c0.at[k - 1], r_c0.at[k - 1], dp, away(k)).start()
    for k in (1, 2, 3):
        to(own_piece(xx, yy), piece(fs, xx, yy), s_r0.at[k - 1], r_r0.at[k - 1], dp, away(k)).start()
    to(rot_h, rfull.at[rows_of(fs), :], s_rx.at[0], r_rx.at[0], dp, other).start()

    def block(c):
        return pl.ds(pl.multiple_of(c * MSG, MSG), MSG)

    def send_block(j, _):
        peer = (dp + j) % NDP
        to(wout.at[peer], win.at[dp], s_meta, r_meta, peer, fs).start()
        to(outb.at[block(peer), :], inb.at[block(dp), :], s_frames, r_frames, peer, fs).start()
        return 0

    lax.fori_loop(1, 22, send_block, 0)
    own = pltpu.make_async_copy(outb.at[block(dp), :], inb.at[block(dp), :], s_own)
    own.start()

    for k, (n, book) in enumerate(((5, cb1), (6, cb2))):
        loads[n].wait()
        value = book[...]
        high = value.astype(BF16)
        cbcat[k * 256 : (k + 1) * 256, 0:128] = high
        cbcat[k * 256 : (k + 1) * 256, 128:256] = (value - high.astype(F32)).astype(BF16)

    def look_up(f, n):
        table = codes[f].astype(F32).T
        entry = iota((128, 256), 1, F32)

        def hot(c):
            return jnp.where(table[:, c : c + 1] == entry, 1.0, 0.0).astype(BF16)

        hots = jnp.concatenate(
            [
                jnp.concatenate([hot(t * 8 + q), hot(t * 8 + 3 + q)], axis=1)
                for t in range(12)
                for q in range(3)
            ],
            axis=0,
        )
        found = jnp.dot(hots, cbcat[...], preferred_element_type=F32)
        found = (found[:, :128] + found[:, 128:]).astype(BF16)
        for t in range(12):
            for q in range(3):
                at = (t * 3 + q) * 128
                deq[t * 128 : (t + 1) * 128, pl.ds(pl.multiple_of(f * SEG + q * 128, 128), 128)] = found[at : at + 128]
        to(deq.at[:, cols_of(f)], deq.at[:, cols_of(f)], s_dx.at[n], r_dx.at[n], dp, other).start()

    look_up(fs, 0)

    for k in (1, 2, 3):
        wait_for(code_piece(back(k), xx), r_c0.at[k - 1])
        for d in (1, 2, 3):
            peer = zlo * 16 + ((xx + d) % 4) * 4 + yy
            to(code_piece(back(k), xx), code_piece(back(k), xx), s_c1, r_c1.at[k - 1], peer, fs).start()
    for k in (1, 2, 3):
        wait_for(piece(back(k), xx, yy), r_r0.at[k - 1])
        for d in (1, 2, 3):
            nx = (xx + d * (1 - core)) % 4
            ny = (yy + d * core) % 4
            to(piece(back(k), xx, yy), piece(back(k), xx, yy), s_r1, r_r1.at[k - 1], zlo * 16 + nx * 4 + ny, fs).start()

    lax.fori_loop(22, 43, send_block, 0)

    for k in (1, 2):
        wait_for(codes.at[0, 0:96, :], r_c1.at[k - 1])
        look_up(back(k), k)

    for k in (1, 2, 3):
        wait_for(rfull.at[0:144, 0:PC], r_r1.at[k - 1])

        def spread(n, _):
            d, m = n // 4 + 1, n % 4
            nx = (xx + d * core) % 4
            ny = (yy + d * (1 - core)) % 4
            px = m * (1 - core) + xx * core
            py = yy * (1 - core) + m * core
            to(piece(back(k), px, py), piece(back(k), px, py), s_r2, r_r2.at[k - 1], zlo * 16 + nx * 4 + ny, fs).start()
            return 0

        lax.fori_loop(0, 12, spread, 0)

    lax.fori_loop(43, NDP, send_block, 0)

    wait_for(codes.at[0, 0:96, :], r_c1.at[2])
    look_up(back(3), 3)
    loads[10].wait()

    for k in (1, 2, 3):
        wait_for(rfull.at[0:576, 0:PC], r_r2.at[k - 1])
        to(rfull.at[rows_of(back(k)), :], rfull.at[rows_of(back(k)), :], s_rx.at[k], r_rx.at[k], dp, other).start()

    wait_for(win.at[0 : NDP - 1], r_meta)
    wait_for(inb.at[0 : (NDP - 1) * MSG, :], r_frames)
    own.wait()
    meta = win[...]
    mask_row = jnp.sum(meta, axis=0) - 1.0
    src_row = jnp.sum(jnp.where(meta > 0.5, iota((NDP, 1, ROWS), 0, F32), 0.0), axis=0)
    eye = iota((ROWS, ROWS), 0) == iota((ROWS, ROWS), 1)
    live = jnp.sum(jnp.where(eye, mask_row, 0.0), axis=1, keepdims=True)
    src = jnp.sum(jnp.where(eye, src_row, 0.0), axis=1, keepdims=True)
    first = src * float(MSG) + (iota((ROWS, 1), 0) % 4).astype(F32)
    for s in range(4):
        put = jnp.where(iota((ROWS, NDP * MSG), 1, F32) == first + 4.0 * s, 1.0, 0.0).astype(BF16)
        xhat[:, s * SEG : (s + 1) * SEG] = jnp.dot(put, inb[...], preferred_element_type=F32)
    xval = xhat[...]
    centered = xval - jnp.sum(xval, axis=1, keepdims=True) * (1.0 / D)
    inv = lax.rsqrt(jnp.sum(centered * centered, axis=1, keepdims=True) * (1.0 / D) + 1e-06)
    standard = centered * inv
    xhat[...] = standard
    loads[7].wait()
    gain_row = gain[...].reshape(1, D)
    normed[...] = (standard * gain_row).astype(BF16)

    for k in range(4):
        wait_for(rfull.at[rows_of(other_of(back(k))), :], r_rx.at[k])

    def forward_u(n, _):
        cols = pl.ds(pl.multiple_of(n * 512, 512), 512)
        ubuf[:, cols] = jnp.dot(normed[...], rfull[:, cols], preferred_element_type=F32).astype(BF16)
        return 0

    lax.fori_loop(0, 3, forward_u, 0)

    loads[8].wait()
    loads[9].wait()
    for k in range(4):
        wait_for(deq.at[:, cols_of(other_of(back(k)))], r_dx.at[k])
    vacc[...] = jnp.zeros_like(vacc)
    nt = (((1,), (1,)), ((), ()))
    for n in range(FF // WIDE):
        cols = slice(n * WIDE, (n + 1) * WIDE)
        inner = jnp.dot(ubuf[...], deq[:, cols], preferred_element_type=F32)
        sc = scale[:, cols]
        pre = inner * sc
        sig = 1.0 / (1.0 + jnp.exp(-pre))
        act[:, cols] = (pre * sig * live).astype(BF16)
        dpre = cot[:, cols].astype(F32) * live * sig * (1.0 + pre * (1.0 - sig))
        part = jnp.sum(dpre * inner, axis=0, keepdims=True)
        sbuf[2 * n] = part[:, :SEG]
        sbuf[2 * n + 1] = part[:, SEG:]
        dinner = (dpre * sc).astype(BF16)
        vacc[...] += lax.dot_general(dinner, deq[:, cols], nt, preferred_element_type=F32)

    sgot[fs] = sbuf[fs]

    def sums_a(j, _):
        pf = (fs + j) % NF
        to(sbuf.at[pf], sgot.at[fs], s_red.at[0], r_red.at[0], dp, pf).start()
        return 0

    lax.fori_loop(1, NF, sums_a, 0)
    act_out = pltpu.make_async_copy(act, act_h, s_out.at[0])
    act_out.start()

    vbuf[...] = vacc[...].astype(BF16)

    def backward_n(n, _):
        rows = pl.ds(pl.multiple_of(n * 512, 512), 512)
        dnorm[:, rows] = lax.dot_general(vbuf[...], rfull[rows, :], nt, preferred_element_type=F32)
        return 0

    lax.fori_loop(0, 3, backward_n, 0)

    dn = dnorm[...]
    xh = xhat[...]
    gpart = jnp.sum(dn * xh, axis=0, keepdims=True)
    ghalf[0] = gpart[:, :HALF]
    ghalf[1] = gpart[:, HALF:]
    to(ghalf.at[1 - core], ggot, s_red.at[3], r_red.at[3], dp, other).start()

    wait_for(sgot.at[0 : NF - 1], r_red.at[0])
    total = jnp.sum(sgot[...], axis=0)
    smsg_b[...] = total
    sgot_b[xy] = total

    def sums_b(j, _):
        to(smsg_b, sgot_b.at[xy], s_red.at[1], r_red.at[1], zlo * 16 + (xy + j) % 16, fs).start()
        return 0

    lax.fori_loop(1, 16, sums_b, 0)

    wait_for(ggot, r_red.at[3])
    total = ghalf[core] + ggot[...]
    gmsg_z[...] = total
    ggot_z[zz] = total

    def gains_z(j, _):
        pz = (zz + j) % 16
        to(gmsg_z, ggot_z.at[zz], s_red.at[4], r_red.at[4], (pz % 4) * 16 + xy, (pz // 4) * 2 + core).start()
        return 0

    lax.fori_loop(1, 16, gains_z, 0)

    dx = dn * gain_row
    m1 = jnp.sum(dx, axis=1, keepdims=True) * (1.0 / D)
    m2 = jnp.sum(dx * xh, axis=1, keepdims=True) * (1.0 / D)
    mfg[...] = (inv * (dx - m1 - xh * m2)).astype(BF16)
    mfg_out = pltpu.make_async_copy(mfg, mfg_h, s_out.at[1])
    mfg_out.start()

    wait_for(ggot_z.at[0:15], r_red.at[4])
    total = jnp.sum(ggot_z[...], axis=0)
    gmsg_x[...] = total
    ggot_x[xy] = total

    def gains_x(j, _):
        to(gmsg_x, ggot_x.at[xy], s_red.at[5], r_red.at[5], zlo * 16 + (xy + j) % 16, fs).start()
        return 0

    lax.fori_loop(1, 16, gains_x, 0)

    wait_for(sgot_b.at[0:15], r_red.at[1])
    total = jnp.sum(sgot_b[...], axis=0)
    smsg_c[...] = total
    sgot_c[zlo] = total
    for j in (1, 2, 3):
        to(smsg_c, sgot_c.at[zlo], s_red.at[2], r_red.at[2], ((zlo + j) % 4) * 16 + xy, fs).start()

    wait_for(ggot_x.at[0:15], r_red.at[5])
    gfin[core] = jnp.sum(ggot_x[...], axis=0)
    to(gfin.at[core], gfin.at[core], s_red.at[6], r_red.at[6], dp, other).start()

    wait_for(outb.at[0 : (NDP - 1) * MSG, :], s_frames)
    wait_for(wout.at[0 : NDP - 1], s_meta)
    for k in range(3):
        wait_for(code_piece(fs, xx), s_c0.at[k])
        wait_for(own_piece(xx, yy), s_r0.at[k])
    wait_for(codes.at[0:3, 0:96, :], s_c1)
    for k in range(4):
        wait_for(rfull.at[0:192, :], s_rx.at[k])
        wait_for(deq.at[:, 0:SEG], s_dx.at[k])
    wait_for(rfull.at[0:432, 0:PC], s_r1)
    wait_for(rfull.at[0:432, :], s_r2)
    wait_for(sgot.at[0 : NF - 1], s_red.at[0])
    wait_for(sgot_b.at[0:15], s_red.at[1])
    wait_for(ghalf.at[0], s_red.at[3])
    wait_for(ggot_z.at[0:15], s_red.at[4])
    wait_for(ggot_x.at[0:15], s_red.at[5])
    act_out.wait()
    mfg_out.wait()

    wait_for(sgot_c.at[0:3], r_red.at[2])
    sred[...] = jnp.sum(sgot_c[...], axis=0)
    wait_for(sgot_c.at[0:3], s_red.at[2])
    wait_for(gfin.at[0], r_red.at[6])
    gred[:, :HALF] = gfin[0]
    gred[:, HALF:] = gfin[1]
    wait_for(gfin.at[0], s_red.at[6])


def finish(act, mfg, sred, gred, act_o, mfg_o, s_o, g_o, sems):
    copies = []
    for n in range(4):
        copies.append(pltpu.make_async_copy(act.at[n * 32 : (n + 1) * 32], act_o.at[n * 32 : (n + 1) * 32], sems.at[n]))
    for n in range(2):
        copies.append(pltpu.make_async_copy(mfg.at[n * 64 : (n + 1) * 64], mfg_o.at[n * 64 : (n + 1) * 64], sems.at[4 + n]))
    for copy in copies:
        copy.start()
    s_o[...] = sred[...].reshape(384)
    g_o[...] = gred[...].reshape(D)
    for copy in copies:
        copy.wait()


def body(
    frames, frame_mask, block_dest, codes_first, codes_second, codebook_first, codebook_second,
    rotation, gain, scale, cotangent,
):
    dma = pltpu.SemaphoreType.DMA
    vm = pltpu.VMEM
    shape = jax.ShapeDtypeStruct
    hbm = pl.BlockSpec(memory_space=pltpu.HBM)
    vmem = pl.BlockSpec(memory_space=pltpu.VMEM)
    act, mfg, sred, gred = pl.pallas_call(
        kernel,
        out_shape=(shape((ROWS, FF), BF16), shape((ROWS, D), BF16), shape((1, 384), F32), shape((1, D), F32)),
        in_specs=[hbm] * 11,
        out_specs=(hbm, hbm, vmem, vmem),
        scratch_shapes=[
            vm((ROWS, D), BF16), vm((ROWS,), jnp.int32), vm((32,), jnp.int32),
            vm((3, D), jnp.int32), vm((3, D), jnp.int32), vm((256, 128), F32), vm((256, 128), F32),
            vm((D,), F32), vm((1, FF), F32), vm((ROWS, FF), BF16), vm((ROWS, FF), BF16), vm((ROWS, D), BF16),
            vm((NDP * MSG, SEG), BF16), vm((NDP * MSG, SEG), BF16),
            vm((NDP, 1, ROWS), F32), vm((NDP, 1, ROWS), F32),
            vm((128, 128), F32), vm((NF, 128, 128), BF16), vm((512, 256), BF16),
            vm((D, D), BF16), vm((D, FF), BF16),
            vm((ROWS, D), F32), vm((ROWS, D), BF16), vm((ROWS, D), BF16),
            vm((ROWS, D), F32), vm((ROWS, D), BF16), vm((ROWS, D), F32),
            vm((NF, 1, SEG), F32), vm((NF, 1, SEG), F32),
            vm((1, SEG), F32), vm((16, 1, SEG), F32), vm((1, SEG), F32), vm((4, 1, SEG), F32),
            vm((2, 1, HALF), F32), vm((1, HALF), F32), vm((1, HALF), F32), vm((16, 1, HALF), F32),
            vm((1, HALF), F32), vm((16, 1, HALF), F32), vm((2, 1, HALF), F32),
            dma((11,)), dma((2,)), dma, dma, dma, dma, dma, dma((3,)), dma((3,)), dma, dma((3,)),
            dma((3,)), dma((3,)), dma, dma((3,)), dma, dma((3,)), dma((4,)), dma((4,)), dma((4,)), dma((4,)),
            dma((7,)), dma((7,)),
        ],
        compiler_params=pltpu.CompilerParams(
            collective_id=0, has_side_effects=True, vmem_limit_bytes=56 * 1024 * 1024
        ),
        cost_estimate=pl.CostEstimate(flops=9_000_000_000, bytes_accessed=8_000_000, transcendentals=400_000),
    )(
        frames, frame_mask, block_dest, codes_first.T, codes_second.T, codebook_first, codebook_second, rotation,
        gain, scale[None, :], cotangent,
    )
    return pl.pallas_call(
        finish,
        out_shape=(shape((ROWS, FF), BF16), shape((ROWS, D), BF16), shape((384,), F32), shape((D,), F32)),
        in_specs=[hbm, hbm, vmem, vmem],
        out_specs=(hbm, hbm, vmem, vmem),
        scratch_shapes=[dma((6,))],
    )(act, mfg, sred, gred)


def solution(mesh):
    rows = P(("dp", "fsdp"), None)
    flat = P(("dp", "fsdp"))
    placed = (
        rows, flat, flat, P(None, "fsdp"), P(None, "fsdp"), P(), P(), P("fsdp", None), P(), P(), rows,
    )
    return jax.shard_map(
        body,
        mesh=mesh,
        in_specs=placed,
        out_specs=(rows, rows, P("fsdp"), P()),
        check_vma=False,
    )
```

```python
import jax
import jax.numpy as jnp
from jax import lax
from jax.experimental import pallas as pl
from jax.experimental.pallas import tpu as pltpu
from jax.sharding import PartitionSpec as P

MESH = pl.DeviceIdType.MESH
F32 = jnp.float32
BF16 = jnp.bfloat16
NDP, NF = 64, 8
ROWS, D, FF = 128, 1536, 3072
SEG = 384
MSG = 16
PR, PC = 48, 384
HALF = D // 2
WIDE = 768


def iota(shape, dim, dtype=jnp.int32):
    found = lax.broadcasted_iota(jnp.int32, shape, dim)
    return found if dtype == jnp.int32 else found.astype(dtype)


def kernel(
    frames_h, mask_h, dest_h, c1_h, c2_h, cb1_h, cb2_h, rot_h, gain_h, scale_h, cot_h,
    act_h, mfg_h, sred, gred,
    frames, mask, destv, c1, c2, cb1, cb2, gain, scale, cot, act, mfg,
    outb, inb, wout, win, codef, codes, cbcat, rfull, deq, xhat, normed, ubuf, vacc, vbuf, dnorm,
    sbuf, sgot, smsg_b, sgot_b, smsg_c, sgot_c, ghalf, ggot_x, gmsg_z, ggot_z, gfin,
    s_in, s_out, s_frames, r_frames, s_meta, r_meta, s_own, s_c0, r_c0, s_c1, r_c1,
    s_r0, r_r0, s_r1, r_r1, s_r2, r_r2, s_rx, r_rx, s_dx, r_dx, s_red, r_red,
):
    dp = lax.axis_index("dp")
    fs = lax.axis_index("fsdp")
    zlo, xy = dp // 16, dp % 16
    xx, yy = xy // 4, xy % 4
    zhi, core = fs // 2, fs % 2
    zz = zhi * 4 + zlo
    other = zhi * 2 + 1 - core

    def to(src, dst, send, recv, d, f):
        return pltpu.make_async_remote_copy(
            src_ref=src, dst_ref=dst, send_sem=send, recv_sem=recv,
            device_id=(d, f), device_id_type=MESH,
        )

    def wait_for(ref, sem):
        pltpu.make_async_copy(ref, ref, sem).wait()

    def rows_of(f):
        return pl.ds(pl.multiple_of(f * 192, 192), 192)

    def cols_of(f):
        return pl.ds(pl.multiple_of(f * SEG, SEG), SEG)

    pairs = (
        (dest_h, destv), (mask_h, mask), (frames_h, frames), (c1_h, c1), (c2_h, c2), (cb1_h, cb1), (cb2_h, cb2),
        (gain_h, gain), (scale_h, scale), (cot_h, cot), (rot_h, rfull.at[rows_of(fs), :]),
    )
    loads = [pltpu.make_async_copy(a, b, s_in.at[n]) for n, (a, b) in enumerate(pairs)]
    for load in loads:
        load.start()

    barrier = pltpu.get_barrier_semaphore()

    def greet(d, f):
        pl.semaphore_signal(barrier, inc=1, device_id=(d, f), device_id_type=MESH)

    def hello_dp(j, _):
        greet((dp + j) % NDP, fs)
        return 0

    def hello_fs(j, _):
        greet(dp, (fs + j) % NF)
        return 0

    def hello_z(j, _):
        greet(((zlo + 1 + j % 3) % 4) * 16 + xy, ((zhi + 1 + j // 3) % 4) * 2 + core)
        return 0

    lax.fori_loop(1, NF, hello_fs, 0)
    lax.fori_loop(1, NDP, hello_dp, 0)
    lax.fori_loop(0, 9, hello_z, 0)

    def hello_x(j, _):
        greet(zlo * 16 + (xy + j) % 16, other)
        return 0

    lax.fori_loop(1, 16, hello_x, 0)

    codef[...] = jnp.zeros_like(codef)
    loads[3].wait()
    loads[4].wait()
    for t in range(12):
        codef[t * 8 : t * 8 + 3, :] = c1[:, t * 128 : (t + 1) * 128].astype(F32)
        codef[t * 8 + 3 : t * 8 + 6, :] = c2[:, t * 128 : (t + 1) * 128].astype(F32)
    codes[fs] = codef[...].astype(BF16)

    loads[0].wait()
    loads[1].wait()
    spread4 = jnp.where(iota((32, ROWS), 1) // 4 == iota((32, ROWS), 0), 1.0, 0.0).astype(BF16)
    dest8 = jnp.broadcast_to(destv[...].reshape(1, 32).astype(F32), (8, 32)).astype(BF16)
    dest = jnp.dot(dest8, spread4, preferred_element_type=F32)[0:1, :].astype(jnp.int32)
    mask_in = mask[...].reshape(1, ROWS).astype(F32)
    lane = iota((1, ROWS), 1)
    key = jnp.concatenate([dest * MSG + s * 4 + lane % 4 for s in range(4)], axis=1)
    wout[...] = jnp.where(iota((NDP, 1, ROWS), 0) == dest[None], 1.0 + mask_in[None], 0.0)
    win[dp] = wout[dp]
    loads[2].wait()
    wide = jnp.concatenate([frames[:, s * SEG : (s + 1) * SEG] for s in range(4)], axis=0)

    def fill(k, _):
        row = iota((256, 4 * ROWS), 0) + k * 256
        pick = jnp.where(row == key, 1.0, 0.0).astype(BF16)
        outb[pl.ds(pl.multiple_of(k * 256, 256), 256), :] = jnp.dot(
            pick, wide, preferred_element_type=F32
        ).astype(BF16)
        return 0

    lax.fori_loop(0, 4, fill, 0)

    pl.semaphore_wait(barrier, NDP - 1 + NF - 1 + 9 + 15)

    def piece(f, i, j):
        return rfull.at[
            pl.ds(pl.multiple_of(f * 192 + i * PR, 16), PR), pl.ds(pl.multiple_of(j * PC, 128), PC)
        ]

    def own_piece(i, j):
        return rot_h.at[pl.ds(pl.multiple_of(i * PR, 16), PR), pl.ds(pl.multiple_of(j * PC, 128), PC)]

    def code_piece(f, i):
        return codes.at[f, pl.ds(pl.multiple_of(i * 32, 32), 32), :]

    def away(k):
        return ((zhi + k) % 4) * 2 + core

    def back(k):
        return ((zhi + 4 - k) % 4) * 2 + core

    def other_of(f):
        return f + 1 - 2 * core

    for k in (2, 1, 3):
        to(code_piece(fs, xx), code_piece(fs, xx), s_c0.at[k - 1], r_c0.at[k - 1], dp, away(k)).start()
    for k in (2, 1, 3):
        to(own_piece(xx, yy), piece(fs, xx, yy), s_r0.at[k - 1], r_r0.at[k - 1], dp, away(k)).start()
    to(rot_h, rfull.at[rows_of(fs), :], s_rx.at[0], r_rx.at[0], dp, other).start()

    def block(c):
        return pl.ds(pl.multiple_of(c * MSG, MSG), MSG)

    def send_block(j, _):
        peer = (dp + j) % NDP
        to(wout.at[peer], win.at[dp], s_meta, r_meta, peer, fs).start()
        to(outb.at[block(peer), :], inb.at[block(dp), :], s_frames, r_frames, peer, fs).start()
        return 0

    lax.fori_loop(1, 22, send_block, 0)
    own = pltpu.make_async_copy(outb.at[block(dp), :], inb.at[block(dp), :], s_own)
    own.start()

    for k, (n, book) in enumerate(((5, cb1), (6, cb2))):
        loads[n].wait()
        value = book[...]
        high = value.astype(BF16)
        cbcat[k * 256 : (k + 1) * 256, 0:128] = high
        cbcat[k * 256 : (k + 1) * 256, 128:256] = (value - high.astype(F32)).astype(BF16)

    def look_up(f, n):
        table = codes[f].astype(F32).T
        entry = iota((128, 256), 1, F32)

        def hot(c):
            return jnp.where(table[:, c : c + 1] == entry, 1.0, 0.0).astype(BF16)

        hots = jnp.concatenate(
            [
                jnp.concatenate([hot(t * 8 + q), hot(t * 8 + 3 + q)], axis=1)
                for t in range(12)
                for q in range(3)
            ],
            axis=0,
        )
        found = jnp.dot(hots, cbcat[...], preferred_element_type=F32)
        found = (found[:, :128] + found[:, 128:]).astype(BF16)
        for t in range(12):
            for q in range(3):
                at = (t * 3 + q) * 128
                deq[t * 128 : (t + 1) * 128, pl.ds(pl.multiple_of(f * SEG + q * 128, 128), 128)] = found[at : at + 128]
        to(deq.at[:, cols_of(f)], deq.at[:, cols_of(f)], s_dx.at[n], r_dx.at[n], dp, other).start()

    look_up(fs, 0)

    for k in (1, 3, 2):
        wait_for(code_piece(back(k), xx), r_c0.at[k - 1])
        for d in (1, 2, 3):
            peer = zlo * 16 + ((xx + d) % 4) * 4 + yy
            to(code_piece(back(k), xx), code_piece(back(k), xx), s_c1, r_c1.at[k - 1], peer, fs).start()
    for k in (1, 3, 2):
        wait_for(piece(back(k), xx, yy), r_r0.at[k - 1])
        for d in (1, 2, 3):
            nx = (xx + d * (1 - core)) % 4
            ny = (yy + d * core) % 4
            to(piece(back(k), xx, yy), piece(back(k), xx, yy), s_r1, r_r1.at[k - 1], zlo * 16 + nx * 4 + ny, fs).start()
        for d in (1, 2, 3):
            nx = (xx + d * core) % 4
            ny = (yy + d * (1 - core)) % 4
            to(piece(back(k), xx, yy), piece(back(k), xx, yy), s_r2, r_r2.at[k - 1], zlo * 16 + nx * 4 + ny, fs).start()

    lax.fori_loop(22, 43, send_block, 0)

    for k in (1, 3):
        wait_for(codes.at[0, 0:96, :], r_c1.at[k - 1])
        look_up(back(k), k)

    for k in (1, 3, 2):
        wait_for(rfull.at[0:144, 0:PC], r_r1.at[k - 1])

        def spread(n, _):
            d = n // 3 + 1
            m = (xx * (1 - core) + yy * core + 1 + n % 3) % 4
            nx = (xx + d * core) % 4
            ny = (yy + d * (1 - core)) % 4
            px = m * (1 - core) + xx * core
            py = yy * (1 - core) + m * core
            to(piece(back(k), px, py), piece(back(k), px, py), s_r2, r_r2.at[k - 1], zlo * 16 + nx * 4 + ny, fs).start()
            return 0

        lax.fori_loop(0, 9, spread, 0)

    lax.fori_loop(43, NDP, send_block, 0)

    wait_for(codes.at[0, 0:96, :], r_c1.at[1])
    look_up(back(2), 2)
    loads[10].wait()

    for k in (1, 3, 2):
        wait_for(rfull.at[0:576, 0:PC], r_r2.at[k - 1])
        to(rfull.at[rows_of(back(k)), :], rfull.at[rows_of(back(k)), :], s_rx.at[k], r_rx.at[k], dp, other).start()

    wait_for(win.at[0 : NDP - 1], r_meta)
    wait_for(inb.at[0 : (NDP - 1) * MSG, :], r_frames)
    own.wait()
    meta = win[...]
    mask_row = jnp.sum(meta, axis=0) - 1.0
    src_row = jnp.sum(jnp.where(meta > 0.5, iota((NDP, 1, ROWS), 0, F32), 0.0), axis=0)
    eye = iota((ROWS, ROWS), 0) == iota((ROWS, ROWS), 1)
    live = jnp.sum(jnp.where(eye, mask_row, 0.0), axis=1, keepdims=True)
    src = jnp.sum(jnp.where(eye, src_row, 0.0), axis=1, keepdims=True)
    first = src * float(MSG) + (iota((ROWS, 1), 0) % 4).astype(F32)
    for s in range(4):
        put = jnp.where(iota((ROWS, NDP * MSG), 1, F32) == first + 4.0 * s, 1.0, 0.0).astype(BF16)
        xhat[:, s * SEG : (s + 1) * SEG] = jnp.dot(put, inb[...], preferred_element_type=F32)
    xval = xhat[...]
    centered = xval - jnp.sum(xval, axis=1, keepdims=True) * (1.0 / D)
    inv = lax.rsqrt(jnp.sum(centered * centered, axis=1, keepdims=True) * (1.0 / D) + 1e-06)
    standard = centered * inv
    xhat[...] = standard
    loads[7].wait()
    gain_row = gain[...].reshape(1, D)
    normed[...] = (standard * gain_row).astype(BF16)

    for k in range(4):
        wait_for(rfull.at[rows_of(other_of(back(k))), :], r_rx.at[k])

    def forward_u(n, _):
        cols = pl.ds(pl.multiple_of(n * 512, 512), 512)
        ubuf[:, cols] = jnp.dot(normed[...], rfull[:, cols], preferred_element_type=F32).astype(BF16)
        return 0

    lax.fori_loop(0, 3, forward_u, 0)

    loads[8].wait()
    loads[9].wait()
    for k in range(4):
        wait_for(deq.at[:, cols_of(other_of(back(k)))], r_dx.at[k])
    vacc[...] = jnp.zeros_like(vacc)
    nt = (((1,), (1,)), ((), ()))
    for n in range(FF // WIDE):
        cols = slice(n * WIDE, (n + 1) * WIDE)
        inner = jnp.dot(ubuf[...], deq[:, cols], preferred_element_type=F32)
        sc = scale[:, cols]
        pre = inner * sc
        sig = 1.0 / (1.0 + jnp.exp(-pre))
        act[:, cols] = (pre * sig * live).astype(BF16)
        dpre = cot[:, cols].astype(F32) * live * sig * (1.0 + pre * (1.0 - sig))
        part = jnp.sum(dpre * inner, axis=0, keepdims=True)
        sbuf[2 * n] = part[:, :SEG]
        sbuf[2 * n + 1] = part[:, SEG:]
        dinner = (dpre * sc).astype(BF16)
        vacc[...] += lax.dot_general(dinner, deq[:, cols], nt, preferred_element_type=F32)

    sgot[fs] = sbuf[fs]

    def sums_a(j, _):
        pf = (fs + j) % NF
        to(sbuf.at[pf], sgot.at[fs], s_red.at[0], r_red.at[0], dp, pf).start()
        return 0

    lax.fori_loop(1, NF, sums_a, 0)
    act_out = pltpu.make_async_copy(act, act_h, s_out.at[0])
    act_out.start()

    vbuf[...] = vacc[...].astype(BF16)

    def backward_n(n, _):
        rows = pl.ds(pl.multiple_of(n * 512, 512), 512)
        dnorm[:, rows] = lax.dot_general(vbuf[...], rfull[rows, :], nt, preferred_element_type=F32)
        return 0

    lax.fori_loop(0, 3, backward_n, 0)

    dn = dnorm[...]
    xh = xhat[...]
    gpart = jnp.sum(dn * xh, axis=0, keepdims=True)
    ghalf[0] = gpart[:, :HALF]
    ghalf[1] = gpart[:, HALF:]
    place = core * 16 + xy
    ggot_x[place] = ghalf[core]

    def gains_x(j, _):
        peer = zlo * 16 + (xy + j) % 16
        to(ghalf.at[1 - core], ggot_x.at[place], s_red.at[3], r_red.at[3], peer, other).start()
        return 0

    def gains_x_own(j, _):
        peer = zlo * 16 + (xy + j) % 16
        to(ghalf.at[core], ggot_x.at[place], s_red.at[3], r_red.at[3], peer, fs).start()
        return 0

    lax.fori_loop(0, 16, gains_x, 0)
    lax.fori_loop(1, 16, gains_x_own, 0)

    dx = dn * gain_row
    m1 = jnp.sum(dx, axis=1, keepdims=True) * (1.0 / D)
    m2 = jnp.sum(dx * xh, axis=1, keepdims=True) * (1.0 / D)
    mfg[...] = (inv * (dx - m1 - xh * m2)).astype(BF16)
    mfg_out = pltpu.make_async_copy(mfg, mfg_h, s_out.at[1])
    mfg_out.start()

    wait_for(sgot.at[0 : NF - 1], r_red.at[0])
    total = jnp.sum(sgot[...], axis=0)
    smsg_b[...] = total
    sgot_b[xy] = total

    def sums_b(j, _):
        to(smsg_b, sgot_b.at[xy], s_red.at[1], r_red.at[1], zlo * 16 + (xy + j) % 16, fs).start()
        return 0

    lax.fori_loop(1, 16, sums_b, 0)

    wait_for(ggot_x.at[0:31], r_red.at[3])
    total = jnp.sum(ggot_x[...], axis=0)
    gmsg_z[...] = total
    ggot_z[zz] = total

    def gains_z(j, _):
        pz = (zz + j) % 16
        to(gmsg_z, ggot_z.at[zz], s_red.at[4], r_red.at[4], (pz % 4) * 16 + xy, (pz // 4) * 2 + core).start()
        return 0

    lax.fori_loop(1, 16, gains_z, 0)

    wait_for(sgot_b.at[0:15], r_red.at[1])
    total = jnp.sum(sgot_b[...], axis=0)
    smsg_c[...] = total
    sgot_c[zlo] = total
    for j in (1, 2, 3):
        to(smsg_c, sgot_c.at[zlo], s_red.at[2], r_red.at[2], ((zlo + j) % 4) * 16 + xy, fs).start()

    wait_for(outb.at[0 : (NDP - 1) * MSG, :], s_frames)
    wait_for(wout.at[0 : NDP - 1], s_meta)
    for k in range(3):
        wait_for(code_piece(fs, xx), s_c0.at[k])
        wait_for(own_piece(xx, yy), s_r0.at[k])
    wait_for(codes.at[0:3, 0:96, :], s_c1)
    for k in range(4):
        wait_for(rfull.at[0:192, :], s_rx.at[k])
        wait_for(deq.at[:, 0:SEG], s_dx.at[k])
    wait_for(rfull.at[0:432, 0:PC], s_r1)
    wait_for(rfull.at[0:432, :], s_r2)
    wait_for(sgot.at[0 : NF - 1], s_red.at[0])
    wait_for(sgot_b.at[0:15], s_red.at[1])
    wait_for(ggot_x.at[0:31], s_red.at[3])
    act_out.wait()
    mfg_out.wait()

    wait_for(ggot_z.at[0:15], r_red.at[4])
    gfin[core] = jnp.sum(ggot_z[...], axis=0)
    to(gfin.at[core], gfin.at[core], s_red.at[5], r_red.at[5], dp, other).start()
    wait_for(ggot_z.at[0:15], s_red.at[4])

    wait_for(sgot_c.at[0:3], r_red.at[2])
    sred[...] = jnp.sum(sgot_c[...], axis=0)
    wait_for(sgot_c.at[0:3], s_red.at[2])
    wait_for(gfin.at[0], r_red.at[5])
    gred[:, :HALF] = gfin[0]
    gred[:, HALF:] = gfin[1]
    wait_for(gfin.at[0], s_red.at[5])


def finish(act, mfg, sred, gred, act_o, mfg_o, s_o, g_o, act_v, mfg_v, sems):
    steps = []
    for n in range(4):
        at = pl.ds(n * 32, 32)
        steps.append((act.at[at], act_v.at[at], act_o.at[at]))
    for n in range(2):
        at = pl.ds(n * 64, 64)
        steps.append((mfg.at[at], mfg_v.at[at], mfg_o.at[at]))
    ins = [pltpu.make_async_copy(a, v, sems.at[n]) for n, (a, v, _) in enumerate(steps)]
    outs = [pltpu.make_async_copy(v, o, sems.at[len(steps) + n]) for n, (_, v, o) in enumerate(steps)]
    for copy in ins:
        copy.start()
    s_o[...] = sred[...].reshape(384)
    g_o[...] = gred[...].reshape(D)
    for arrive, leave in zip(ins, outs):
        arrive.wait()
        leave.start()
    for copy in outs:
        copy.wait()


def body(
    frames, frame_mask, block_dest, codes_first, codes_second, codebook_first, codebook_second,
    rotation, gain, scale, cotangent,
):
    dma = pltpu.SemaphoreType.DMA
    vm = pltpu.VMEM
    shape = jax.ShapeDtypeStruct
    hbm = pl.BlockSpec(memory_space=pltpu.HBM)
    vmem = pl.BlockSpec(memory_space=pltpu.VMEM)
    act, mfg, sred, gred = pl.pallas_call(
        kernel,
        out_shape=(shape((ROWS, FF), BF16), shape((ROWS, D), BF16), shape((1, 384), F32), shape((1, D), F32)),
        in_specs=[hbm] * 11,
        out_specs=(hbm, hbm, vmem, vmem),
        scratch_shapes=[
            vm((ROWS, D), BF16), vm((ROWS,), jnp.int32), vm((32,), jnp.int32),
            vm((3, D), jnp.int32), vm((3, D), jnp.int32), vm((256, 128), F32), vm((256, 128), F32),
            vm((D,), F32), vm((1, FF), F32), vm((ROWS, FF), BF16), vm((ROWS, FF), BF16), vm((ROWS, D), BF16),
            vm((NDP * MSG, SEG), BF16), vm((NDP * MSG, SEG), BF16),
            vm((NDP, 1, ROWS), F32), vm((NDP, 1, ROWS), F32),
            vm((128, 128), F32), vm((NF, 128, 128), BF16), vm((512, 256), BF16),
            vm((D, D), BF16), vm((D, FF), BF16),
            vm((ROWS, D), F32), vm((ROWS, D), BF16), vm((ROWS, D), BF16),
            vm((ROWS, D), F32), vm((ROWS, D), BF16), vm((ROWS, D), F32),
            vm((NF, 1, SEG), F32), vm((NF, 1, SEG), F32),
            vm((1, SEG), F32), vm((16, 1, SEG), F32), vm((1, SEG), F32), vm((4, 1, SEG), F32),
            vm((2, 1, HALF), F32), vm((32, 1, HALF), F32), vm((1, HALF), F32), vm((16, 1, HALF), F32),
            vm((2, 1, HALF), F32),
            dma((11,)), dma((2,)), dma, dma, dma, dma, dma, dma((3,)), dma((3,)), dma, dma((3,)),
            dma((3,)), dma((3,)), dma, dma((3,)), dma, dma((3,)), dma((4,)), dma((4,)), dma((4,)), dma((4,)),
            dma((6,)), dma((6,)),
        ],
        compiler_params=pltpu.CompilerParams(
            collective_id=0, has_side_effects=True, vmem_limit_bytes=56 * 1024 * 1024
        ),
        cost_estimate=pl.CostEstimate(flops=9_000_000_000, bytes_accessed=8_000_000, transcendentals=400_000),
    )(
        frames, frame_mask, block_dest, codes_first.T, codes_second.T, codebook_first, codebook_second, rotation,
        gain, scale[None, :], cotangent,
    )
    return pl.pallas_call(
        finish,
        out_shape=(shape((ROWS, FF), BF16), shape((ROWS, D), BF16), shape((384,), F32), shape((D,), F32)),
        in_specs=[hbm, hbm, vmem, vmem],
        out_specs=(hbm, hbm, vmem, vmem),
        scratch_shapes=[vm((ROWS, FF), BF16), vm((ROWS, D), BF16), dma((12,))],
    )(act, mfg, sred, gred)


def solution(mesh):
    rows = P(("dp", "fsdp"), None)
    flat = P(("dp", "fsdp"))
    placed = (
        rows, flat, flat, P(None, "fsdp"), P(None, "fsdp"), P(), P(), P("fsdp", None), P(), P(), rows,
    )
    return jax.shard_map(
        body,
        mesh=mesh,
        in_specs=placed,
        out_specs=(rows, rows, P("fsdp"), P()),
        check_vma=False,
    )
```

```python
import jax
import jax.numpy as jnp
from jax import lax
from jax.experimental import pallas as pl
from jax.experimental.pallas import tpu as pltpu
from jax.sharding import PartitionSpec as P

MESH = pl.DeviceIdType.MESH
F32 = jnp.float32
BF16 = jnp.bfloat16
NDP, NF = 64, 8
ROWS, D, FF = 128, 1536, 3072
SEG = 384
MSG = 16
PR, PC = 48, 384
HALF = D // 2
WIDE = 768


def iota(shape, dim, dtype=jnp.int32):
    found = lax.broadcasted_iota(jnp.int32, shape, dim)
    return found if dtype == jnp.int32 else found.astype(dtype)


def kernel(
    frames_h, mask_h, dest_h, c1_h, c2_h, cb1_h, cb2_h, rot_h, gain_h, scale_h, cot_h,
    act_h, mfg_h, sred_h, gred_h,
    frames, mask, destv, c1, c2, cb1, cb2, gain, scale, cot, act, mfg, sred, gred,
    outb, inb, wout, win, put, codef, codes, cbcat, rfull, deq, xhat, normed, ubuf, vacc, vbuf, dnorm,
    sbuf, sgot, smsg_b, sgot_b, smsg_c, sgot_c, ghalf, ggot_x, gmsg_z, ggot_z, gfin,
    s_in, s_out, s_frames, r_frames, s_meta, r_meta, s_own, s_c0, r_c0, s_c1, r_c1,
    s_r0, r_r0, s_r1, r_r1, s_r2, r_r2, s_rx, r_rx, s_dx, r_dx, s_red, r_red,
):
    dp = lax.axis_index("dp")
    fs = lax.axis_index("fsdp")
    zlo, xy = dp // 16, dp % 16
    xx, yy = xy // 4, xy % 4
    zhi, core = fs // 2, fs % 2
    zz = zhi * 4 + zlo
    other = zhi * 2 + 1 - core

    def to(src, dst, send, recv, d, f):
        return pltpu.make_async_remote_copy(
            src_ref=src, dst_ref=dst, send_sem=send, recv_sem=recv,
            device_id=(d, f), device_id_type=MESH,
        )

    def wait_for(ref, sem):
        pltpu.make_async_copy(ref, ref, sem).wait()

    def rows_of(f):
        return pl.ds(pl.multiple_of(f * 192, 192), 192)

    def cols_of(f):
        return pl.ds(pl.multiple_of(f * SEG, SEG), SEG)

    pairs = (
        (dest_h, destv), (mask_h, mask), (frames_h, frames), (c1_h, c1), (c2_h, c2), (cb1_h, cb1), (cb2_h, cb2),
        (gain_h, gain), (scale_h, scale), (cot_h, cot), (rot_h, rfull.at[rows_of(fs), :]),
    )
    loads = [pltpu.make_async_copy(a, b, s_in.at[n]) for n, (a, b) in enumerate(pairs)]
    for load in loads:
        load.start()

    barrier = pltpu.get_barrier_semaphore()

    def greet(d, f):
        pl.semaphore_signal(barrier, inc=1, device_id=(d, f), device_id_type=MESH)

    def hello_dp(j, _):
        greet((dp + j) % NDP, fs)
        return 0

    def hello_fs(j, _):
        greet(dp, (fs + j) % NF)
        return 0

    def hello_z(j, _):
        greet(((zlo + 1 + j % 3) % 4) * 16 + xy, ((zhi + 1 + j // 3) % 4) * 2 + core)
        return 0

    lax.fori_loop(1, NF, hello_fs, 0)
    lax.fori_loop(1, NDP, hello_dp, 0)
    lax.fori_loop(0, 9, hello_z, 0)

    def hello_x(j, _):
        greet(zlo * 16 + (xy + j) % 16, other)
        return 0

    lax.fori_loop(1, 16, hello_x, 0)

    codef[...] = jnp.zeros_like(codef)
    loads[3].wait()
    loads[4].wait()
    for t in range(12):
        codef[t * 8 : t * 8 + 3, :] = c1[:, t * 128 : (t + 1) * 128].astype(F32)
        codef[t * 8 + 3 : t * 8 + 6, :] = c2[:, t * 128 : (t + 1) * 128].astype(F32)
    codes[fs] = codef[...].astype(BF16)

    loads[0].wait()
    loads[1].wait()
    spread4 = jnp.where(iota((32, ROWS), 1) // 4 == iota((32, ROWS), 0), 1.0, 0.0).astype(BF16)
    dest8 = jnp.broadcast_to(destv[...].reshape(1, 32).astype(F32), (8, 32)).astype(BF16)
    dest = jnp.dot(dest8, spread4, preferred_element_type=F32)[0:1, :].astype(jnp.int32)
    mask_in = mask[...].reshape(1, ROWS).astype(F32)
    lane = iota((1, ROWS), 1)
    key = jnp.concatenate([dest * MSG + s * 4 + lane % 4 for s in range(4)], axis=1)
    wout[...] = jnp.where(iota((NDP, 1, ROWS), 0) == dest[None], 1.0 + mask_in[None], 0.0)
    win[dp] = wout[dp]
    loads[2].wait()
    wide = jnp.concatenate([frames[:, s * SEG : (s + 1) * SEG] for s in range(4)], axis=0)

    def fill(k, _):
        row = iota((256, 4 * ROWS), 0) + k * 256
        pick = jnp.where(row == key, 1.0, 0.0).astype(BF16)
        outb[pl.ds(pl.multiple_of(k * 256, 256), 256), :] = jnp.dot(
            pick, wide, preferred_element_type=F32
        ).astype(BF16)
        return 0

    lax.fori_loop(0, 4, fill, 0)

    pl.semaphore_wait(barrier, NDP - 1 + NF - 1 + 9 + 15)

    def piece(f, i, j):
        return rfull.at[
            pl.ds(pl.multiple_of(f * 192 + i * PR, 16), PR), pl.ds(pl.multiple_of(j * PC, 128), PC)
        ]

    def own_piece(i, j):
        return rot_h.at[pl.ds(pl.multiple_of(i * PR, 16), PR), pl.ds(pl.multiple_of(j * PC, 128), PC)]

    def code_piece(f, i):
        return codes.at[f, pl.ds(pl.multiple_of(i * 32, 32), 32), :]

    def away(k):
        return ((zhi + k) % 4) * 2 + core

    def back(k):
        return ((zhi + 4 - k) % 4) * 2 + core

    def other_of(f):
        return f + 1 - 2 * core

    for k in (2, 1, 3):
        to(code_piece(fs, xx), code_piece(fs, xx), s_c0.at[k - 1], r_c0.at[k - 1], dp, away(k)).start()
    for k in (2, 1, 3):
        to(own_piece(xx, yy), piece(fs, xx, yy), s_r0.at[k - 1], r_r0.at[k - 1], dp, away(k)).start()
    to(rot_h, rfull.at[rows_of(fs), :], s_rx.at[0], r_rx.at[0], dp, other).start()

    def block(c):
        return pl.ds(pl.multiple_of(c * MSG, MSG), MSG)

    def send_block(j, _):
        peer = (dp + j) % NDP
        to(outb.at[block(peer), :], inb.at[block(dp), :], s_frames, r_frames, peer, fs).start()
        return 0

    def send_meta(j, _):
        peer = (dp + j) % NDP
        to(wout.at[peer], win.at[dp], s_meta, r_meta, peer, fs).start()
        return 0

    lax.fori_loop(1, 22, send_block, 0)
    lax.fori_loop(1, NDP, send_meta, 0)
    own = pltpu.make_async_copy(outb.at[block(dp), :], inb.at[block(dp), :], s_own)
    own.start()

    for k, (n, book) in enumerate(((5, cb1), (6, cb2))):
        loads[n].wait()
        value = book[...]
        high = value.astype(BF16)
        cbcat[k * 256 : (k + 1) * 256, 0:128] = high
        cbcat[k * 256 : (k + 1) * 256, 128:256] = (value - high.astype(F32)).astype(BF16)

    def look_up(f, n):
        table = codes[f].astype(F32).T
        entry = iota((128, 256), 1, F32)

        def hot(c):
            return jnp.where(table[:, c : c + 1] == entry, 1.0, 0.0).astype(BF16)

        hots = jnp.concatenate(
            [
                jnp.concatenate([hot(t * 8 + q), hot(t * 8 + 3 + q)], axis=1)
                for t in range(12)
                for q in range(3)
            ],
            axis=0,
        )
        found = jnp.dot(hots, cbcat[...], preferred_element_type=F32)
        found = (found[:, :128] + found[:, 128:]).astype(BF16)
        for t in range(12):
            for q in range(3):
                at = (t * 3 + q) * 128
                deq[t * 128 : (t + 1) * 128, pl.ds(pl.multiple_of(f * SEG + q * 128, 128), 128)] = found[at : at + 128]
        to(deq.at[:, cols_of(f)], deq.at[:, cols_of(f)], s_dx.at[n], r_dx.at[n], dp, other).start()

    look_up(fs, 0)

    def pass_codes(k):
        wait_for(code_piece(back(k), xx), r_c0.at[k - 1])
        for d in (1, 2, 3):
            peer = zlo * 16 + ((xx + d) % 4) * 4 + yy
            to(code_piece(back(k), xx), code_piece(back(k), xx), s_c1, r_c1.at[k - 1], peer, fs).start()

    def pass_piece(k):
        mine = piece(back(k), xx, yy)
        wait_for(mine, r_r0.at[k - 1])
        for d in (1, 2, 3):
            nx = (xx + d * (1 - core)) % 4
            ny = (yy + d * core) % 4
            to(mine, mine, s_r1, r_r1.at[k - 1], zlo * 16 + nx * 4 + ny, fs).start()
        for d in (1, 2, 3):
            nx = (xx + d * core) % 4
            ny = (yy + d * (1 - core)) % 4
            to(mine, mine, s_r2, r_r2.at[k - 1], zlo * 16 + nx * 4 + ny, fs).start()

    def pass_line(k):
        wait_for(rfull.at[0:144, 0:PC], r_r1.at[k - 1])

        def spread(n, _):
            d = n // 3 + 1
            m = (xx * (1 - core) + yy * core + 1 + n % 3) % 4
            nx = (xx + d * core) % 4
            ny = (yy + d * (1 - core)) % 4
            px = m * (1 - core) + xx * core
            py = yy * (1 - core) + m * core
            to(piece(back(k), px, py), piece(back(k), px, py), s_r2, r_r2.at[k - 1], zlo * 16 + nx * 4 + ny, fs).start()
            return 0

        lax.fori_loop(0, 9, spread, 0)

    pass_piece(1)
    pass_piece(3)
    pass_codes(1)
    pass_codes(3)
    lax.fori_loop(22, 43, send_block, 0)
    pass_piece(2)
    pass_codes(2)
    pass_line(1)
    pass_line(3)
    lax.fori_loop(43, NDP, send_block, 0)
    pass_line(2)

    for k in (1, 3, 2):
        wait_for(codes.at[0, 0:96, :], r_c1.at[k - 1])
        look_up(back(k), k)

    wait_for(win.at[0 : NDP - 1], r_meta)
    meta = win[...]
    mask_row = jnp.sum(meta, axis=0) - 1.0
    src_row = jnp.sum(jnp.where(meta > 0.5, iota((NDP, 1, ROWS), 0, F32), 0.0), axis=0)
    eye = iota((ROWS, ROWS), 0) == iota((ROWS, ROWS), 1)
    live = jnp.sum(jnp.where(eye, mask_row, 0.0), axis=1, keepdims=True)
    src = jnp.sum(jnp.where(eye, src_row, 0.0), axis=1, keepdims=True)
    first = src * float(MSG) + (iota((ROWS, 1), 0) % 4).astype(F32)
    for s in range(4):
        put[s] = jnp.where(iota((ROWS, NDP * MSG), 1, F32) == first + 4.0 * s, 1.0, 0.0).astype(BF16)

    loads[10].wait()

    for k in (1, 3, 2):
        wait_for(rfull.at[0:576, 0:PC], r_r2.at[k - 1])
        to(rfull.at[rows_of(back(k)), :], rfull.at[rows_of(back(k)), :], s_rx.at[k], r_rx.at[k], dp, other).start()

    wait_for(inb.at[0 : (NDP - 1) * MSG, :], r_frames)
    own.wait()
    for s in range(4):
        xhat[:, s * SEG : (s + 1) * SEG] = jnp.dot(put[s], inb[...], preferred_element_type=F32)
    xval = xhat[...]
    centered = xval - jnp.sum(xval, axis=1, keepdims=True) * (1.0 / D)
    inv = lax.rsqrt(jnp.sum(centered * centered, axis=1, keepdims=True) * (1.0 / D) + 1e-06)
    standard = centered * inv
    xhat[...] = standard
    loads[7].wait()
    gain_row = gain[...].reshape(1, D)
    normed[...] = (standard * gain_row).astype(BF16)

    for k in range(4):
        wait_for(rfull.at[rows_of(other_of(back(k))), :], r_rx.at[k])

    def forward_u(n, _):
        cols = pl.ds(pl.multiple_of(n * 512, 512), 512)
        ubuf[:, cols] = jnp.dot(normed[...], rfull[:, cols], preferred_element_type=F32).astype(BF16)
        return 0

    lax.fori_loop(0, 3, forward_u, 0)

    loads[8].wait()
    loads[9].wait()
    for k in range(4):
        wait_for(deq.at[:, cols_of(other_of(back(k)))], r_dx.at[k])
    vacc[...] = jnp.zeros_like(vacc)
    nt = (((1,), (1,)), ((), ()))
    for n in range(FF // WIDE):
        cols = slice(n * WIDE, (n + 1) * WIDE)
        inner = jnp.dot(ubuf[...], deq[:, cols], preferred_element_type=F32)
        sc = scale[:, cols]
        pre = inner * sc
        sig = 1.0 / (1.0 + jnp.exp(-pre))
        act[:, cols] = (pre * sig * live).astype(BF16)
        dpre = cot[:, cols].astype(F32) * live * sig * (1.0 + pre * (1.0 - sig))
        part = jnp.sum(dpre * inner, axis=0, keepdims=True)
        sbuf[2 * n] = part[:, :SEG]
        sbuf[2 * n + 1] = part[:, SEG:]
        dinner = (dpre * sc).astype(BF16)
        vacc[...] += lax.dot_general(dinner, deq[:, cols], nt, preferred_element_type=F32)

    sgot[fs] = sbuf[fs]

    def sums_a(j, _):
        pf = (fs + j) % NF
        to(sbuf.at[pf], sgot.at[fs], s_red.at[0], r_red.at[0], dp, pf).start()
        return 0

    lax.fori_loop(1, NF, sums_a, 0)
    act_out = pltpu.make_async_copy(act, act_h, s_out.at[0])
    act_out.start()

    vbuf[...] = vacc[...].astype(BF16)

    def backward_n(n, _):
        rows = pl.ds(pl.multiple_of(n * 512, 512), 512)
        dnorm[:, rows] = lax.dot_general(vbuf[...], rfull[rows, :], nt, preferred_element_type=F32)
        return 0

    lax.fori_loop(0, 3, backward_n, 0)

    dn = dnorm[...]
    xh = xhat[...]
    gpart = jnp.sum(dn * xh, axis=0, keepdims=True)
    ghalf[0] = gpart[:, :HALF]
    ghalf[1] = gpart[:, HALF:]
    place = core * 16 + xy
    ggot_x[place] = ghalf[core]

    def gains_x(j, _):
        peer = zlo * 16 + (xy + j) % 16
        to(ghalf.at[1 - core], ggot_x.at[place], s_red.at[3], r_red.at[3], peer, other).start()
        return 0

    def gains_x_own(j, _):
        peer = zlo * 16 + (xy + j) % 16
        to(ghalf.at[core], ggot_x.at[place], s_red.at[3], r_red.at[3], peer, fs).start()
        return 0

    lax.fori_loop(0, 16, gains_x, 0)
    lax.fori_loop(1, 16, gains_x_own, 0)

    dx = dn * gain_row
    m1 = jnp.sum(dx, axis=1, keepdims=True) * (1.0 / D)
    m2 = jnp.sum(dx * xh, axis=1, keepdims=True) * (1.0 / D)
    mfg[...] = (inv * (dx - m1 - xh * m2)).astype(BF16)
    mfg_out = pltpu.make_async_copy(mfg, mfg_h, s_out.at[1])
    mfg_out.start()

    wait_for(sgot.at[0 : NF - 1], r_red.at[0])
    total = jnp.sum(sgot[...], axis=0)
    smsg_b[...] = total
    sgot_b[xy] = total

    def sums_b(j, _):
        to(smsg_b, sgot_b.at[xy], s_red.at[1], r_red.at[1], zlo * 16 + (xy + j) % 16, fs).start()
        return 0

    lax.fori_loop(1, 16, sums_b, 0)

    wait_for(ggot_x.at[0:31], r_red.at[3])
    total = jnp.sum(ggot_x[...], axis=0)
    gmsg_z[...] = total
    ggot_z[zz] = total

    def gains_z(j, _):
        pz = (zz + j) % 16
        to(gmsg_z, ggot_z.at[zz], s_red.at[4], r_red.at[4], (pz % 4) * 16 + xy, (pz // 4) * 2 + core).start()
        return 0

    lax.fori_loop(1, 16, gains_z, 0)

    wait_for(sgot_b.at[0:15], r_red.at[1])
    total = jnp.sum(sgot_b[...], axis=0)
    smsg_c[...] = total
    sgot_c[zlo] = total
    for j in (1, 2, 3):
        to(smsg_c, sgot_c.at[zlo], s_red.at[2], r_red.at[2], ((zlo + j) % 4) * 16 + xy, fs).start()

    wait_for(outb.at[0 : (NDP - 1) * MSG, :], s_frames)
    wait_for(wout.at[0 : NDP - 1], s_meta)
    for k in range(3):
        wait_for(code_piece(fs, xx), s_c0.at[k])
        wait_for(own_piece(xx, yy), s_r0.at[k])
    wait_for(codes.at[0:3, 0:96, :], s_c1)
    for k in range(4):
        wait_for(rfull.at[0:192, :], s_rx.at[k])
        wait_for(deq.at[:, 0:SEG], s_dx.at[k])
    wait_for(rfull.at[0:432, 0:PC], s_r1)
    wait_for(rfull.at[0:432, :], s_r2)
    wait_for(sgot.at[0 : NF - 1], s_red.at[0])
    wait_for(sgot_b.at[0:15], s_red.at[1])
    wait_for(ggot_x.at[0:31], s_red.at[3])
    act_out.wait()
    mfg_out.wait()

    wait_for(ggot_z.at[0:15], r_red.at[4])
    gfin[core] = jnp.sum(ggot_z[...], axis=0)
    to(gfin.at[core], gfin.at[core], s_red.at[5], r_red.at[5], dp, other).start()
    wait_for(ggot_z.at[0:15], s_red.at[4])

    wait_for(sgot_c.at[0:3], r_red.at[2])
    sred[...] = jnp.sum(sgot_c[...], axis=0)
    sred_out = pltpu.make_async_copy(sred, sred_h, s_out.at[2])
    sred_out.start()
    wait_for(sgot_c.at[0:3], s_red.at[2])
    wait_for(gfin.at[0], r_red.at[5])
    gred[:, :HALF] = gfin[0]
    gred[:, HALF:] = gfin[1]
    gred_out = pltpu.make_async_copy(gred, gred_h, s_out.at[3])
    gred_out.start()
    sred_out.wait()
    gred_out.wait()
    wait_for(gfin.at[0], s_red.at[5])


def finish(act, mfg, sred, gred, act_o, mfg_o, s_o, g_o, act_v, mfg_v, s_v, g_v, s1, g1, sems):
    steps = []
    for n in range(4):
        at = pl.ds(n * 32, 32)
        steps.append((act.at[at], act_v.at[at], act_o.at[at]))
    for n in range(2):
        at = pl.ds(n * 64, 64)
        steps.append((mfg.at[at], mfg_v.at[at], mfg_o.at[at]))
    steps.append((sred, s_v, None))
    steps.append((gred, g_v, None))
    ins = [pltpu.make_async_copy(a, v, sems.at[n]) for n, (a, v, _) in enumerate(steps)]
    for copy in ins:
        copy.start()
    outs = []
    for n in (6, 7, 0, 1, 2, 3, 4, 5):
        ins[n].wait()
        if n == 6:
            s1[...] = s_v[...].reshape(384)
            leave = pltpu.make_async_copy(s1, s_o, sems.at[8 + n])
        elif n == 7:
            g1[...] = g_v[...].reshape(D)
            leave = pltpu.make_async_copy(g1, g_o, sems.at[8 + n])
        else:
            leave = pltpu.make_async_copy(steps[n][1], steps[n][2], sems.at[8 + n])
        leave.start()
        outs.append(leave)
    for copy in outs:
        copy.wait()


def body(
    frames, frame_mask, block_dest, codes_first, codes_second, codebook_first, codebook_second,
    rotation, gain, scale, cotangent,
):
    dma = pltpu.SemaphoreType.DMA
    vm = pltpu.VMEM
    shape = jax.ShapeDtypeStruct
    hbm = pl.BlockSpec(memory_space=pltpu.HBM)
    act, mfg, sred, gred = pl.pallas_call(
        kernel,
        out_shape=(shape((ROWS, FF), BF16), shape((ROWS, D), BF16), shape((1, 384), F32), shape((1, D), F32)),
        in_specs=[hbm] * 11,
        out_specs=(hbm, hbm, hbm, hbm),
        scratch_shapes=[
            vm((ROWS, D), BF16), vm((ROWS,), jnp.int32), vm((32,), jnp.int32),
            vm((3, D), jnp.int32), vm((3, D), jnp.int32), vm((256, 128), F32), vm((256, 128), F32),
            vm((D,), F32), vm((1, FF), F32), vm((ROWS, FF), BF16), vm((ROWS, FF), BF16), vm((ROWS, D), BF16), vm((1, 384), F32), vm((1, D), F32),
            vm((NDP * MSG, SEG), BF16), vm((NDP * MSG, SEG), BF16),
            vm((NDP, 1, ROWS), F32), vm((NDP, 1, ROWS), F32), vm((4, ROWS, NDP * MSG), BF16),
            vm((128, 128), F32), vm((NF, 128, 128), BF16), vm((512, 256), BF16),
            vm((D, D), BF16), vm((D, FF), BF16),
            vm((ROWS, D), F32), vm((ROWS, D), BF16), vm((ROWS, D), BF16),
            vm((ROWS, D), F32), vm((ROWS, D), BF16), vm((ROWS, D), F32),
            vm((NF, 1, SEG), F32), vm((NF, 1, SEG), F32),
            vm((1, SEG), F32), vm((16, 1, SEG), F32), vm((1, SEG), F32), vm((4, 1, SEG), F32),
            vm((2, 1, HALF), F32), vm((32, 1, HALF), F32), vm((1, HALF), F32), vm((16, 1, HALF), F32),
            vm((2, 1, HALF), F32),
            dma((11,)), dma((4,)), dma, dma, dma, dma, dma, dma((3,)), dma((3,)), dma, dma((3,)),
            dma((3,)), dma((3,)), dma, dma((3,)), dma, dma((3,)), dma((4,)), dma((4,)), dma((4,)), dma((4,)),
            dma((6,)), dma((6,)),
        ],
        compiler_params=pltpu.CompilerParams(
            collective_id=0, has_side_effects=True, vmem_limit_bytes=56 * 1024 * 1024
        ),
        cost_estimate=pl.CostEstimate(flops=9_000_000_000, bytes_accessed=8_000_000, transcendentals=400_000),
    )(
        frames, frame_mask, block_dest, codes_first.T, codes_second.T, codebook_first, codebook_second, rotation,
        gain, scale[None, :], cotangent,
    )
    return pl.pallas_call(
        finish,
        out_shape=(shape((ROWS, FF), BF16), shape((ROWS, D), BF16), shape((384,), F32), shape((D,), F32)),
        in_specs=[hbm] * 4,
        out_specs=(hbm,) * 4,
        scratch_shapes=[
            vm((ROWS, FF), BF16), vm((ROWS, D), BF16), vm((1, 384), F32), vm((1, D), F32), vm((384,), F32), vm((D,), F32),
            dma((16,)),
        ],
        compiler_params=pltpu.CompilerParams(vmem_limit_bytes=56 * 1024 * 1024),
    )(act, mfg, sred, gred)


def solution(mesh):
    rows = P(("dp", "fsdp"), None)
    flat = P(("dp", "fsdp"))
    placed = (
        rows, flat, flat, P(None, "fsdp"), P(None, "fsdp"), P(), P(), P("fsdp", None), P(), P(), rows,
    )
    return jax.shard_map(
        body,
        mesh=mesh,
        in_specs=placed,
        out_specs=(rows, rows, P("fsdp"), P()),
        check_vma=False,
    )
```

```python
import jax
import jax.numpy as jnp
from jax import lax
from jax.experimental import pallas as pl
from jax.experimental.pallas import tpu as pltpu
from jax.sharding import PartitionSpec as P

MESH = pl.DeviceIdType.MESH
F32 = jnp.float32
BF16 = jnp.bfloat16
NDP, NF = 64, 8
ROWS, D, FF = 128, 1536, 3072
SEG = 384
MSG = 16
PR, PC = 48, 384
HALF = D // 2
WIDE = 768


def iota(shape, dim, dtype=jnp.int32):
    found = lax.broadcasted_iota(jnp.int32, shape, dim)
    return found if dtype == jnp.int32 else found.astype(dtype)


def kernel(
    frames_h, mask_h, dest_h, c1_h, c2_h, cb1_h, cb2_h, rot_h, gain_h, scale_h, cot_h,
    act_h, mfg_h, sred_h, gred_h,
    frames, mask, destv, c1, c2, cb1, cb2, gain, scale, cot, act, mfg, sred, gred,
    outb, inb, wout, win, put, codef, codes, cbcat, rfull, deq, xhat, normed, ubuf, vacc, vbuf, dnorm,
    sbuf, sgot, smsg_b, sgot_b, smsg_c, sgot_c, ghalf, ggot_x, gmsg_z, ggot_z, gfin,
    s_in, s_out, s_frames, r_frames, s_meta, r_meta, s_own, s_c0, r_c0, s_c1, r_c1,
    s_r0, r_r0, s_r1, r_r1, s_r2, r_r2, s_rx, r_rx, s_dx, r_dx, s_red, r_red,
):
    dp = lax.axis_index("dp")
    fs = lax.axis_index("fsdp")
    zlo, xy = dp // 16, dp % 16
    xx, yy = xy // 4, xy % 4
    zhi, core = fs // 2, fs % 2
    zz = zhi * 4 + zlo
    other = zhi * 2 + 1 - core

    def to(src, dst, send, recv, d, f):
        return pltpu.make_async_remote_copy(
            src_ref=src, dst_ref=dst, send_sem=send, recv_sem=recv,
            device_id=(d, f), device_id_type=MESH,
        )

    def wait_for(ref, sem):
        pltpu.make_async_copy(ref, ref, sem).wait()

    def rows_of(f):
        return pl.ds(pl.multiple_of(f * 192, 192), 192)

    def cols_of(f):
        return pl.ds(pl.multiple_of(f * SEG, SEG), SEG)

    pairs = (
        (dest_h, destv), (mask_h, mask), (frames_h, frames), (c1_h, c1), (c2_h, c2), (cb1_h, cb1), (cb2_h, cb2),
        (gain_h, gain), (scale_h, scale), (cot_h, cot), (rot_h, rfull.at[rows_of(fs), :]),
    )
    loads = [pltpu.make_async_copy(a, b, s_in.at[n]) for n, (a, b) in enumerate(pairs)]
    for load in loads:
        load.start()

    barrier = pltpu.get_barrier_semaphore()

    def greet(d, f):
        pl.semaphore_signal(barrier, inc=1, device_id=(d, f), device_id_type=MESH)

    def hello_dp(j, _):
        greet((dp + j) % NDP, fs)
        return 0

    def hello_fs(j, _):
        greet(dp, (fs + j) % NF)
        return 0

    def hello_z(j, _):
        greet(((zlo + 1 + j % 3) % 4) * 16 + xy, ((zhi + 1 + j // 3) % 4) * 2 + core)
        return 0

    lax.fori_loop(1, NF, hello_fs, 0)
    lax.fori_loop(1, NDP, hello_dp, 0)
    lax.fori_loop(0, 9, hello_z, 0)

    def hello_x(j, _):
        greet(zlo * 16 + (xy + j) % 16, other)
        return 0

    lax.fori_loop(1, 16, hello_x, 0)

    codef[...] = jnp.zeros_like(codef)
    loads[3].wait()
    loads[4].wait()
    for t in range(12):
        codef[t * 8 : t * 8 + 3, :] = c1[:, t * 128 : (t + 1) * 128].astype(F32)
        codef[t * 8 + 3 : t * 8 + 6, :] = c2[:, t * 128 : (t + 1) * 128].astype(F32)
    codes[fs] = codef[...].astype(BF16)

    loads[0].wait()
    loads[1].wait()
    spread4 = jnp.where(iota((32, ROWS), 1) // 4 == iota((32, ROWS), 0), 1.0, 0.0).astype(BF16)
    dest8 = jnp.broadcast_to(destv[...].reshape(1, 32).astype(F32), (8, 32)).astype(BF16)
    dest = jnp.dot(dest8, spread4, preferred_element_type=F32)[0:1, :].astype(jnp.int32)
    mask_in = mask[...].reshape(1, ROWS).astype(F32)
    lane = iota((1, ROWS), 1)
    key = jnp.concatenate([dest * MSG + s * 4 + lane % 4 for s in range(4)], axis=1)
    wout[...] = jnp.where(iota((NDP, 1, ROWS), 0) == dest[None], 1.0 + mask_in[None], 0.0)
    win[dp] = wout[dp]
    loads[2].wait()
    wide = jnp.concatenate([frames[:, s * SEG : (s + 1) * SEG] for s in range(4)], axis=0)

    def fill(k, _):
        row = iota((256, 4 * ROWS), 0) + k * 256
        pick = jnp.where(row == key, 1.0, 0.0).astype(BF16)
        outb[pl.ds(pl.multiple_of(k * 256, 256), 256), :] = jnp.dot(
            pick, wide, preferred_element_type=F32
        ).astype(BF16)
        return 0

    lax.fori_loop(0, 4, fill, 0)

    pl.semaphore_wait(barrier, NDP - 1 + NF - 1 + 9 + 15)

    def piece(f, i, j):
        return rfull.at[
            pl.ds(pl.multiple_of(f * 192 + i * PR, 16), PR), pl.ds(pl.multiple_of(j * PC, 128), PC)
        ]

    def own_piece(i, j):
        return rot_h.at[pl.ds(pl.multiple_of(i * PR, 16), PR), pl.ds(pl.multiple_of(j * PC, 128), PC)]

    def code_piece(f, i):
        return codes.at[f, pl.ds(pl.multiple_of(i * 32, 32), 32), :]

    def away(k):
        return ((zhi + k) % 4) * 2 + core

    def back(k):
        return ((zhi + 4 - k) % 4) * 2 + core

    def other_of(f):
        return f + 1 - 2 * core

    for k in (2, 1, 3):
        to(code_piece(fs, xx), code_piece(fs, xx), s_c0.at[k - 1], r_c0.at[k - 1], dp, away(k)).start()
    for k in (2, 1, 3):
        to(own_piece(xx, yy), piece(fs, xx, yy), s_r0.at[k - 1], r_r0.at[k - 1], dp, away(k)).start()
    to(rot_h, rfull.at[rows_of(fs), :], s_rx.at[0], r_rx.at[0], dp, other).start()

    def block(c):
        return pl.ds(pl.multiple_of(c * MSG, MSG), MSG)

    def send_block(j, _):
        peer = (dp + j) % NDP
        to(outb.at[block(peer), :], inb.at[block(dp), :], s_frames, r_frames, peer, fs).start()
        return 0

    def send_meta(j, _):
        peer = (dp + j) % NDP
        to(wout.at[peer], win.at[dp], s_meta, r_meta, peer, fs).start()
        return 0

    lax.fori_loop(1, NDP, send_meta, 0)
    lax.fori_loop(1, NDP, send_block, 0)
    own = pltpu.make_async_copy(outb.at[block(dp), :], inb.at[block(dp), :], s_own)
    own.start()

    for k, (n, book) in enumerate(((5, cb1), (6, cb2))):
        loads[n].wait()
        value = book[...]
        high = value.astype(BF16)
        cbcat[k * 256 : (k + 1) * 256, 0:128] = high
        cbcat[k * 256 : (k + 1) * 256, 128:256] = (value - high.astype(F32)).astype(BF16)

    def look_up(f, n):
        table = codes[f].astype(F32).T
        entry = iota((128, 256), 1, F32)

        def hot(c):
            return jnp.where(table[:, c : c + 1] == entry, 1.0, 0.0).astype(BF16)

        hots = jnp.concatenate(
            [
                jnp.concatenate([hot(t * 8 + q), hot(t * 8 + 3 + q)], axis=1)
                for t in range(12)
                for q in range(3)
            ],
            axis=0,
        )
        found = jnp.dot(hots, cbcat[...], preferred_element_type=F32)
        found = (found[:, :128] + found[:, 128:]).astype(BF16)
        for t in range(12):
            for q in range(3):
                at = (t * 3 + q) * 128
                deq[t * 128 : (t + 1) * 128, pl.ds(pl.multiple_of(f * SEG + q * 128, 128), 128)] = found[at : at + 128]
        to(deq.at[:, cols_of(f)], deq.at[:, cols_of(f)], s_dx.at[n], r_dx.at[n], dp, other).start()

    look_up(fs, 0)

    def pass_codes(k):
        wait_for(code_piece(back(k), xx), r_c0.at[k - 1])
        for d in (1, 2, 3):
            peer = zlo * 16 + ((xx + d) % 4) * 4 + yy
            to(code_piece(back(k), xx), code_piece(back(k), xx), s_c1, r_c1.at[k - 1], peer, fs).start()

    def pass_piece(k):
        mine = piece(back(k), xx, yy)
        wait_for(mine, r_r0.at[k - 1])
        for d in (1, 2, 3):
            nx = (xx + d * (1 - core)) % 4
            ny = (yy + d * core) % 4
            to(mine, mine, s_r1, r_r1.at[k - 1], zlo * 16 + nx * 4 + ny, fs).start()
        for d in (1, 2, 3):
            nx = (xx + d * core) % 4
            ny = (yy + d * (1 - core)) % 4
            to(mine, mine, s_r2, r_r2.at[k - 1], zlo * 16 + nx * 4 + ny, fs).start()

    def pass_line(k):
        wait_for(rfull.at[0:144, 0:PC], r_r1.at[k - 1])

        def spread(n, _):
            d = n // 3 + 1
            m = (xx * (1 - core) + yy * core + 1 + n % 3) % 4
            nx = (xx + d * core) % 4
            ny = (yy + d * (1 - core)) % 4
            px = m * (1 - core) + xx * core
            py = yy * (1 - core) + m * core
            to(piece(back(k), px, py), piece(back(k), px, py), s_r2, r_r2.at[k - 1], zlo * 16 + nx * 4 + ny, fs).start()
            return 0

        lax.fori_loop(0, 9, spread, 0)

    pass_codes(1)
    pass_codes(3)
    def pass_far():
        mine = piece(back(2), xx, yy)
        wait_for(mine, r_r0.at[1])

        def direct(j, _):
            to(mine, mine, s_r2, r_r2.at[1], zlo * 16 + (xy + j) % 16, fs).start()
            return 0

        lax.fori_loop(1, 16, direct, 0)

    pass_piece(1)
    pass_piece(3)
    pass_codes(2)
    pass_far()
    for k in (1, 3,):
        wait_for(codes.at[0, 0:96, :], r_c1.at[k - 1])
        look_up(back(k), k)
    pass_line(1)
    pass_line(3)
    for k in (2,):
        wait_for(codes.at[0, 0:96, :], r_c1.at[k - 1])
        look_up(back(k), k)
    wait_for(win.at[0 : NDP - 1], r_meta)
    meta = win[...]
    mask_row = jnp.sum(meta, axis=0) - 1.0
    src_row = jnp.sum(jnp.where(meta > 0.5, iota((NDP, 1, ROWS), 0, F32), 0.0), axis=0)
    eye = iota((ROWS, ROWS), 0) == iota((ROWS, ROWS), 1)
    live = jnp.sum(jnp.where(eye, mask_row, 0.0), axis=1, keepdims=True)
    src = jnp.sum(jnp.where(eye, src_row, 0.0), axis=1, keepdims=True)
    first = src * float(MSG) + (iota((ROWS, 1), 0) % 4).astype(F32)
    for s in range(4):
        put[s] = jnp.where(iota((ROWS, NDP * MSG), 1, F32) == first + 4.0 * s, 1.0, 0.0).astype(BF16)

    loads[10].wait()

    for k in (1, 3, 2):
        count = 720 if k == 2 else 576
        wait_for(rfull.at[0:count, 0:PC], r_r2.at[k - 1])
        to(rfull.at[rows_of(back(k)), :], rfull.at[rows_of(back(k)), :], s_rx.at[k], r_rx.at[k], dp, other).start()

    wait_for(inb.at[0 : (NDP - 1) * MSG, :], r_frames)
    own.wait()
    for s in range(4):
        xhat[:, s * SEG : (s + 1) * SEG] = jnp.dot(put[s], inb[...], preferred_element_type=F32)
    xval = xhat[...]
    centered = xval - jnp.sum(xval, axis=1, keepdims=True) * (1.0 / D)
    inv = lax.rsqrt(jnp.sum(centered * centered, axis=1, keepdims=True) * (1.0 / D) + 1e-06)
    standard = centered * inv
    xhat[...] = standard
    loads[7].wait()
    gain_row = gain[...].reshape(1, D)
    normed[...] = (standard * gain_row).astype(BF16)

    for k in (0, 1, 3, 2):
        wait_for(rfull.at[rows_of(other_of(back(k))), :], r_rx.at[k])
        depth = pl.ds(pl.multiple_of(((zhi + 4 - k) % 4) * 384, 128), 384)
        part = jnp.dot(normed[:, depth], rfull[depth, :], preferred_element_type=F32)
        if k == 0:
            vacc[...] = part
        elif k == 2:
            ubuf[...] = (vacc[...] + part).astype(BF16)
        else:
            vacc[...] += part

    loads[8].wait()
    loads[9].wait()
    for k in range(4):
        wait_for(deq.at[:, cols_of(other_of(back(k)))], r_dx.at[k])
    vacc[...] = jnp.zeros_like(vacc)
    nt = (((1,), (1,)), ((), ()))
    for n in range(FF // WIDE):
        cols = slice(n * WIDE, (n + 1) * WIDE)
        inner = jnp.dot(ubuf[...], deq[:, cols], preferred_element_type=F32)
        sc = scale[:, cols]
        pre = inner * sc
        sig = 1.0 / (1.0 + jnp.exp(-pre))
        act[:, cols] = (pre * sig * live).astype(BF16)
        dpre = cot[:, cols].astype(F32) * live * sig * (1.0 + pre * (1.0 - sig))
        part = jnp.sum(dpre * inner, axis=0, keepdims=True)
        sbuf[2 * n] = part[:, :SEG]
        sbuf[2 * n + 1] = part[:, SEG:]
        dinner = (dpre * sc).astype(BF16)
        vacc[...] += lax.dot_general(dinner, deq[:, cols], nt, preferred_element_type=F32)

    sgot[fs] = sbuf[fs]

    def sums_a(j, _):
        pf = (fs + j) % NF
        to(sbuf.at[pf], sgot.at[fs], s_red.at[0], r_red.at[0], dp, pf).start()
        return 0

    lax.fori_loop(1, NF, sums_a, 0)
    act_out = pltpu.make_async_copy(act, act_h, s_out.at[0])
    act_out.start()

    vbuf[...] = vacc[...].astype(BF16)

    def backward_n(n, _):
        rows = pl.ds(pl.multiple_of(n * 512, 512), 512)
        dnorm[:, rows] = lax.dot_general(vbuf[...], rfull[rows, :], nt, preferred_element_type=F32)
        return 0

    lax.fori_loop(0, 3, backward_n, 0)

    dn = dnorm[...]
    xh = xhat[...]
    gpart = jnp.sum(dn * xh, axis=0, keepdims=True)
    ghalf[0] = gpart[:, :HALF]
    ghalf[1] = gpart[:, HALF:]
    place = core * 16 + xy
    ggot_x[place] = ghalf[core]

    def gains_x(j, _):
        peer = zlo * 16 + (xy + j) % 16
        to(ghalf.at[1 - core], ggot_x.at[place], s_red.at[3], r_red.at[3], peer, other).start()
        return 0

    def gains_x_own(j, _):
        peer = zlo * 16 + (xy + j) % 16
        to(ghalf.at[core], ggot_x.at[place], s_red.at[3], r_red.at[3], peer, fs).start()
        return 0

    lax.fori_loop(0, 16, gains_x, 0)
    lax.fori_loop(1, 16, gains_x_own, 0)

    dx = dn * gain_row
    m1 = jnp.sum(dx, axis=1, keepdims=True) * (1.0 / D)
    m2 = jnp.sum(dx * xh, axis=1, keepdims=True) * (1.0 / D)
    mfg[...] = (inv * (dx - m1 - xh * m2)).astype(BF16)
    mfg_out = pltpu.make_async_copy(mfg, mfg_h, s_out.at[1])
    mfg_out.start()

    wait_for(sgot.at[0 : NF - 1], r_red.at[0])
    total = jnp.sum(sgot[...], axis=0)
    smsg_b[...] = total
    sgot_b[xy] = total

    def sums_b(j, _):
        to(smsg_b, sgot_b.at[xy], s_red.at[1], r_red.at[1], zlo * 16 + (xy + j) % 16, fs).start()
        return 0

    lax.fori_loop(1, 16, sums_b, 0)

    wait_for(ggot_x.at[0:31], r_red.at[3])
    total = jnp.sum(ggot_x[...], axis=0)
    gmsg_z[...] = total
    ggot_z[zz] = total

    def gains_z(j, _):
        pz = (zz + j) % 16
        to(gmsg_z, ggot_z.at[zz], s_red.at[4], r_red.at[4], (pz % 4) * 16 + xy, (pz // 4) * 2 + core).start()
        return 0

    lax.fori_loop(1, 16, gains_z, 0)

    wait_for(sgot_b.at[0:15], r_red.at[1])
    total = jnp.sum(sgot_b[...], axis=0)
    smsg_c[...] = total
    sgot_c[zlo] = total
    for j in (1, 2, 3):
        to(smsg_c, sgot_c.at[zlo], s_red.at[2], r_red.at[2], ((zlo + j) % 4) * 16 + xy, fs).start()

    wait_for(outb.at[0 : (NDP - 1) * MSG, :], s_frames)
    wait_for(wout.at[0 : NDP - 1], s_meta)
    for k in range(3):
        wait_for(code_piece(fs, xx), s_c0.at[k])
        wait_for(own_piece(xx, yy), s_r0.at[k])
    wait_for(codes.at[0:3, 0:96, :], s_c1)
    for k in range(4):
        wait_for(rfull.at[0:192, :], s_rx.at[k])
        wait_for(deq.at[:, 0:SEG], s_dx.at[k])
    wait_for(rfull.at[0:288, 0:PC], s_r1)
    wait_for(rfull.at[0:624, 0:1152], s_r2)
    wait_for(sgot.at[0 : NF - 1], s_red.at[0])
    wait_for(sgot_b.at[0:15], s_red.at[1])
    wait_for(ggot_x.at[0:31], s_red.at[3])
    act_out.wait()
    mfg_out.wait()

    wait_for(ggot_z.at[0:15], r_red.at[4])
    gfin[core] = jnp.sum(ggot_z[...], axis=0)
    to(gfin.at[core], gfin.at[core], s_red.at[5], r_red.at[5], dp, other).start()
    wait_for(ggot_z.at[0:15], s_red.at[4])

    wait_for(sgot_c.at[0:3], r_red.at[2])
    sred[...] = jnp.sum(sgot_c[...], axis=0)
    sred_out = pltpu.make_async_copy(sred, sred_h, s_out.at[2])
    sred_out.start()
    wait_for(sgot_c.at[0:3], s_red.at[2])
    wait_for(gfin.at[0], r_red.at[5])
    gred[:, :HALF] = gfin[0]
    gred[:, HALF:] = gfin[1]
    gred_out = pltpu.make_async_copy(gred, gred_h, s_out.at[3])
    gred_out.start()
    sred_out.wait()
    gred_out.wait()
    wait_for(gfin.at[0], s_red.at[5])


def finish(act, mfg, sred, gred, act_o, mfg_o, s_o, g_o, act_v, mfg_v, s_v, g_v, s1, g1, sems):
    steps = []
    for n in range(4):
        at = pl.ds(n * 32, 32)
        steps.append((act.at[at], act_v.at[at], act_o.at[at]))
    for n in range(2):
        at = pl.ds(n * 64, 64)
        steps.append((mfg.at[at], mfg_v.at[at], mfg_o.at[at]))
    steps.append((sred, s_v, None))
    steps.append((gred, g_v, None))
    ins = [pltpu.make_async_copy(a, v, sems.at[n]) for n, (a, v, _) in enumerate(steps)]
    for copy in ins:
        copy.start()
    outs = []
    for n in (6, 7, 0, 1, 2, 3, 4, 5):
        ins[n].wait()
        if n == 6:
            s1[...] = s_v[...].reshape(384)
            leave = pltpu.make_async_copy(s1, s_o, sems.at[8 + n])
        elif n == 7:
            g1[...] = g_v[...].reshape(D)
            leave = pltpu.make_async_copy(g1, g_o, sems.at[8 + n])
        else:
            leave = pltpu.make_async_copy(steps[n][1], steps[n][2], sems.at[8 + n])
        leave.start()
        outs.append(leave)
    for copy in outs:
        copy.wait()


def body(
    frames, frame_mask, block_dest, codes_first, codes_second, codebook_first, codebook_second,
    rotation, gain, scale, cotangent,
):
    dma = pltpu.SemaphoreType.DMA
    vm = pltpu.VMEM
    shape = jax.ShapeDtypeStruct
    hbm = pl.BlockSpec(memory_space=pltpu.HBM)
    act, mfg, sred, gred = pl.pallas_call(
        kernel,
        out_shape=(shape((ROWS, FF), BF16), shape((ROWS, D), BF16), shape((1, 384), F32), shape((1, D), F32)),
        in_specs=[hbm] * 11,
        out_specs=(hbm, hbm, hbm, hbm),
        scratch_shapes=[
            vm((ROWS, D), BF16), vm((ROWS,), jnp.int32), vm((32,), jnp.int32),
            vm((3, D), jnp.int32), vm((3, D), jnp.int32), vm((256, 128), F32), vm((256, 128), F32),
            vm((D,), F32), vm((1, FF), F32), vm((ROWS, FF), BF16), vm((ROWS, FF), BF16), vm((ROWS, D), BF16), vm((1, 384), F32), vm((1, D), F32),
            vm((NDP * MSG, SEG), BF16), vm((NDP * MSG, SEG), BF16),
            vm((NDP, 1, ROWS), F32), vm((NDP, 1, ROWS), F32), vm((4, ROWS, NDP * MSG), BF16),
            vm((128, 128), F32), vm((NF, 128, 128), BF16), vm((512, 256), BF16),
            vm((D, D), BF16), vm((D, FF), BF16),
            vm((ROWS, D), F32), vm((ROWS, D), BF16), vm((ROWS, D), BF16),
            vm((ROWS, D), F32), vm((ROWS, D), BF16), vm((ROWS, D), F32),
            vm((NF, 1, SEG), F32), vm((NF, 1, SEG), F32),
            vm((1, SEG), F32), vm((16, 1, SEG), F32), vm((1, SEG), F32), vm((4, 1, SEG), F32),
            vm((2, 1, HALF), F32), vm((32, 1, HALF), F32), vm((1, HALF), F32), vm((16, 1, HALF), F32),
            vm((2, 1, HALF), F32),
            dma((11,)), dma((4,)), dma, dma, dma, dma, dma, dma((3,)), dma((3,)), dma, dma((3,)),
            dma((3,)), dma((3,)), dma, dma((3,)), dma, dma((3,)), dma((4,)), dma((4,)), dma((4,)), dma((4,)),
            dma((6,)), dma((6,)),
        ],
        compiler_params=pltpu.CompilerParams(
            collective_id=0, has_side_effects=True, vmem_limit_bytes=56 * 1024 * 1024
        ),
        cost_estimate=pl.CostEstimate(flops=9_000_000_000, bytes_accessed=8_000_000, transcendentals=400_000),
    )(
        frames, frame_mask, block_dest, codes_first.T, codes_second.T, codebook_first, codebook_second, rotation,
        gain, scale[None, :], cotangent,
    )
    return pl.pallas_call(
        finish,
        out_shape=(shape((ROWS, FF), BF16), shape((ROWS, D), BF16), shape((384,), F32), shape((D,), F32)),
        in_specs=[hbm] * 4,
        out_specs=(hbm,) * 4,
        scratch_shapes=[
            vm((ROWS, FF), BF16), vm((ROWS, D), BF16), vm((1, 384), F32), vm((1, D), F32), vm((384,), F32), vm((D,), F32),
            dma((16,)),
        ],
        compiler_params=pltpu.CompilerParams(vmem_limit_bytes=56 * 1024 * 1024),
    )(act, mfg, sred, gred)


def solution(mesh):
    rows = P(("dp", "fsdp"), None)
    flat = P(("dp", "fsdp"))
    placed = (
        rows, flat, flat, P(None, "fsdp"), P(None, "fsdp"), P(), P(), P("fsdp", None), P(), P(), rows,
    )
    return jax.shard_map(
        body,
        mesh=mesh,
        in_specs=placed,
        out_specs=(rows, rows, P("fsdp"), P()),
        check_vma=False,
    )
```
